32 devices in a mesh: engine: 4 (over x, core), fsdp: 4 (over z), tensor: 2 (over y).
Axes of the slice: x: 2, y: 2, z: 4, core: 2. Of those that a mesh axis runs over, the one named last changes fastest.
Arguments:
- layer_input: bfloat16 [2048, 16384], P(('engine', 'fsdp'), 'tensor'), may hold values from -6 to 6
- norm_gain: bfloat16 [16384], P('tensor'), may hold values from 0.099609375 to 1.8984375
- query_base: bfloat16 [16384, 256], P(('engine', 'fsdp'), 'tensor'), may hold values from -0.046875 to 0.046875
- query_down: bfloat16 [16384, 64], P(('engine', 'fsdp')), may hold values from -0.046875 to 0.046875
- query_up: bfloat16 [64, 256], P(None, 'tensor'), may hold values from -0.29882812 to 0.29882812
- kv_base: bfloat16 [2, 8192, 256], P('tensor', ('engine', 'fsdp')), may hold values from -0.046875 to 0.046875
- output_base_weight: bfloat16 [256, 2, 8192], P(None, 'tensor', ('engine', 'fsdp')), may hold values from -0.375 to 0.375
- output_down_factor: bfloat16 [256, 64], P('tensor'), may hold values from -0.375 to 0.375
- output_up_factor: bfloat16 [64, 2, 8192], P(None, 'tensor', ('engine', 'fsdp')), may hold values from -0.29882812 to 0.29882812
- cache_keys: bfloat16 [16, 512, 128], P(('engine', 'fsdp')), may hold values from -250 to 250
- cache_values: bfloat16 [16, 512, 128], P(('engine', 'fsdp')), may hold values from -6 to 6
- positions: int32 [16, 128], P(('engine', 'fsdp')), may hold values from 0 to 767, as said below
- offsets: int32 [16], P(('engine', 'fsdp')), may hold values from 0 to 512, as said below
Outputs:
- attended: bfloat16 [2048, 16384], P(('engine', 'fsdp'), 'tensor')
The draws below stay inside these ranges and needn't reach their ends.
Inputs may be any that keep to these rules, and one draw needn't show every extreme that they name: `offsets`: each group's offset is its count of valid cache slots; some group has 512 and some group has 0. `positions`: positions rise along each group's row, by 1 or 2 a token; the first is its group's offset or one more; the group with 512 valid slots rises by 2 at every token.
All inputs are finite; a program needn't handle non-finite values.
Results may differ from the reference program's by a relative error of at most 0.03.
Values may be sent and summed in bfloat16 or wider, within the bound.
A program may use at most 64 MiB of HBM per device.

```python
import jax
import jax.numpy as jnp
from jax import lax

MODEL_WIDTH = 16384
HEAD = 128
RANK = 64
TOK = 128
CACHE = 512
GROUPS = 16
QHEADS = 2
QUERY_FEATURES = 256
DBLOCK = 8192
TOKENS = 2048
N_TENSOR = 2


def shared_offsets(key):
    counts = jax.random.randint(jax.random.fold_in(key, 11), (GROUPS,), 0, CACHE + 1)
    full_group = jax.random.randint(jax.random.fold_in(key, 12), (), 0, GROUPS)
    empty_group = (full_group + 1 + jax.random.randint(jax.random.fold_in(key, 13), (), 0, GROUPS - 1)) % GROUPS
    counts = counts.at[full_group].set(CACHE)
    counts = counts.at[empty_group].set(0)
    return (counts.astype(jnp.int32), full_group)


def draw_offsets(key, part):
    counts, full_group = shared_offsets(key)
    return counts


def draw_positions(key, part):
    starts, full_group = shared_offsets(key)
    key = jax.random.fold_in(key, 5)
    strides = jax.random.randint(key, (GROUPS, TOK), 1, 3)
    chosen = (jnp.arange(GROUPS) == full_group)[:, None]
    strides = jnp.where(chosen, 2, strides)
    return (starts[:, None] + jnp.cumsum(strides, axis=1) - 1).astype(jnp.int32)


def draw_cache_keys(key, part):
    key = jax.random.fold_in(key, 7)
    base = jnp.clip(jax.random.normal(key, (GROUPS, CACHE, HEAD), jnp.float32), -6.0, 6.0)
    return base.astype(jnp.bfloat16)


def block_levels(stream_key, shape, split, smallest, largest):
    level = 1.0
    for axis_at, blocks in split:
        steps = jax.random.uniform(jax.random.fold_in(jax.random.fold_in(stream_key, 6), axis_at), (blocks,), jnp.float32, smallest / len(split), largest / len(split))
        level = level * jnp.repeat(jnp.exp(steps), shape[axis_at] // blocks).reshape((-1,) + (1,) * (len(shape) - 1 - axis_at))
    return level


def scatter_about(rng, extent, spread, limit, shards=(), kind=jnp.bfloat16):
    values = jax.random.normal(rng, extent, jnp.float32) * spread
    if len(shards) > 0:
        values = block_levels(rng, extent, shards, -0.22, 0.18) * values
    return jnp.clip(values, min=-limit, max=limit).astype(kind)


def setup_inputs(seed: int = 0) -> dict:
    seeds = jax.random.split(jax.random.key(seed), 14)
    return {
        "layer_input": scatter_about(seeds[0], (TOKENS, MODEL_WIDTH), 1.0, 6.0, ((0, 16), (1, 2))),
        "norm_gain": jnp.clip(1.0 + 0.18 * jax.random.normal(seeds[1], (MODEL_WIDTH,), jnp.float32), 0.099609375, 1.8984375).astype(jnp.bfloat16),
        "query_base": scatter_about(seeds[2], (MODEL_WIDTH, QUERY_FEATURES), MODEL_WIDTH ** -0.5, 0.046875, ((0, 16), (1, 2))),
        "query_down": scatter_about(seeds[3], (MODEL_WIDTH, RANK), MODEL_WIDTH ** -0.5, 0.046875, ((0, 16),)),
        "query_up": scatter_about(seeds[4], (RANK, QUERY_FEATURES), 0.05, 0.29882812, ((1, 2),)),
        "kv_base": scatter_about(seeds[5], (N_TENSOR, DBLOCK, 2 * HEAD), MODEL_WIDTH ** -0.5, 0.046875, ((0, 2), (1, 16))),
        "output_base_weight": scatter_about(seeds[6], (QUERY_FEATURES, N_TENSOR, DBLOCK), QUERY_FEATURES ** -0.5, 0.375, ((1, 2), (2, 16))),
        "output_down_factor": scatter_about(seeds[7], (QUERY_FEATURES, RANK), QUERY_FEATURES ** -0.5, 0.375, ((0, 2),)),
        "output_up_factor": scatter_about(seeds[8], (RANK, N_TENSOR, DBLOCK), 0.05, 0.29882812, ((1, 2), (2, 16))),
        "cache_keys": draw_cache_keys(jax.random.fold_in(seeds[13], 71), 0),
        "cache_values": scatter_about(seeds[10], (GROUPS, CACHE, HEAD), 1.0, 6.0, ((0, 16),)),
        "positions": draw_positions(jax.random.fold_in(seeds[13], 71), 0),
        "offsets": draw_offsets(jax.random.fold_in(seeds[13], 71), 0),
    }


def rotate(values, places):
    half = values.shape[-1] // 2
    index = jnp.arange(half).astype(jnp.float32)
    inverse = jnp.exp(index * (-2.0 / values.shape[-1]) * jnp.log(jnp.float32(500000.0)))
    angle = places.astype(jnp.float32)[:, None] * inverse[None, :]
    cosine = jnp.cos(angle)
    sine = jnp.sin(angle)
    first = values[:, :half]
    second = values[:, half:]
    return jnp.concatenate([first * cosine - second * sine, second * cosine + first * sine], axis=1)

def attend(query, new_keys, new_values, old_keys, old_values, offset):
    tok_count = query.shape[0]
    slots = old_keys.shape[0]
    keys_all = jnp.concatenate([old_keys, new_keys], axis=0)
    values_all = jnp.concatenate([old_values, new_values], axis=0)
    scores = jnp.dot(query, keys_all.T, preferred_element_type=jnp.float32) * query.shape[-1] ** (-0.5)
    slot_seen = jnp.broadcast_to(jnp.arange(slots)[None, :] < offset, (tok_count, slots))
    rows = jnp.arange(tok_count)
    new_seen = rows[None, :] <= rows[:, None]
    seen = jnp.concatenate([slot_seen, new_seen], axis=1)
    scores = jnp.where(seen, scores, jnp.float32(-1e+30))
    top = lax.optimization_barrier(jnp.max(scores, axis=1, keepdims=True))
    probs = jnp.exp(scores - top)
    weights = (probs / lax.optimization_barrier(jnp.sum(probs, axis=1, keepdims=True))).astype(jnp.bfloat16)
    return jnp.dot(weights, values_all, preferred_element_type=jnp.float32).astype(jnp.bfloat16)

def reference(layer_input, norm_gain, query_base, query_down, query_up, kv_base, output_base_weight, output_down_factor, output_up_factor, cache_keys, cache_values, positions, offsets):
    query_merged = (query_base.astype(jnp.float32) + 2.0 * jnp.dot(query_down, query_up, preferred_element_type=jnp.float32)).astype(jnp.bfloat16)
    adapter_output_delta = jnp.einsum('lz,zam->lam', output_down_factor.astype(jnp.float32), output_up_factor.astype(jnp.float32))
    output_weight_combined = (output_base_weight.astype(jnp.float32) + 2.0 * adapter_output_delta).astype(jnp.bfloat16).reshape(QUERY_FEATURES, MODEL_WIDTH)
    kv_weight = kv_base.reshape(MODEL_WIDTH, 2 * HEAD)
    inputs = layer_input.reshape(GROUPS, TOK, MODEL_WIDTH)

    def one_group(packed):
        block, old_keys, old_values, places, offset = packed
        wide = block.astype(jnp.float32)
        scale = lax.rsqrt(lax.optimization_barrier(jnp.mean(wide * wide, axis=1, keepdims=True)) + 1e-05)
        normed = (wide * scale * norm_gain.astype(jnp.float32)[None, :]).astype(jnp.bfloat16)
        query_all = jnp.dot(normed, query_merged, preferred_element_type=jnp.float32)
        kv = jnp.dot(normed, kv_weight, preferred_element_type=jnp.float32)
        new_keys = rotate(kv[:, :HEAD], places).astype(jnp.bfloat16)
        new_values = kv[:, HEAD:].astype(jnp.bfloat16)
        total = jnp.zeros((TOK, MODEL_WIDTH), jnp.float32)
        for head in range(QHEADS):
            query = rotate(query_all[:, head * HEAD:(head + 1) * HEAD], places).astype(jnp.bfloat16)
            head_out = attend(query, new_keys, new_values, old_keys, old_values, offset)
            part = jnp.dot(head_out, output_weight_combined[head * HEAD:(head + 1) * HEAD], preferred_element_type=jnp.float32)
            total = total + part.astype(jnp.bfloat16).astype(jnp.float32)
        return total.astype(jnp.bfloat16)
    result = lax.map(one_group, (inputs, cache_keys, cache_values, positions, offsets))
    return result.reshape(TOKENS, MODEL_WIDTH)
```

```python
import functools

import jax
import jax.numpy as jnp
from jax import lax
from jax.experimental import pallas as pl
from jax.experimental.pallas import tpu as pltpu
from jax.sharding import PartitionSpec as P

MESH = pl.DeviceIdType.MESH
KV, QUERY, OUT = 0, 1, 2
SIB, CROSS, LEFT, RIGHT = 0, 1, 2, 3


def rotate(values, places):
    half = values.shape[-1] // 2
    index = jnp.arange(half).astype(jnp.float32)
    inverse = jnp.exp(index * (-2.0 / values.shape[-1]) * jnp.log(jnp.float32(500000.0)))
    angle = places.astype(jnp.float32)[:, None] * inverse[None, :]
    cosine = jnp.cos(angle)
    sine = jnp.sin(angle)
    first = values[:, :half]
    second = values[:, half:]
    return jnp.concatenate([first * cosine - second * sine, second * cosine + first * sine], axis=1)


def attend(query, new_keys, new_values, old_keys, old_values, offset):
    tok_count = query.shape[0]
    slots = old_keys.shape[0]
    keys_all = jnp.concatenate([old_keys, new_keys], axis=0)
    values_all = jnp.concatenate([old_values, new_values], axis=0)
    scores = jnp.dot(query, keys_all.T, preferred_element_type=jnp.float32) * query.shape[-1] ** (
        -0.5
    )
    slot_seen = jnp.broadcast_to(jnp.arange(slots)[None, :] < offset, (tok_count, slots))
    rows = jnp.arange(tok_count)
    new_seen = rows[None, :] <= rows[:, None]
    seen = jnp.concatenate([slot_seen, new_seen], axis=1)
    scores = jnp.where(seen, scores, jnp.float32(-1e30))
    top = jnp.max(scores, axis=1, keepdims=True)
    probs = jnp.exp(scores - top)
    weights = (probs / jnp.sum(probs, axis=1, keepdims=True)).astype(jnp.bfloat16)
    return jnp.dot(weights, values_all, preferred_element_type=jnp.float32).astype(jnp.bfloat16)


def per_device_plain(
    layer_input,
    norm_gain,
    query_base,
    query_down,
    query_up,
    kv_base,
    output_base_weight,
    output_down_factor,
    output_up_factor,
    cache_keys,
    cache_values,
    positions,
    offsets,
):
    head_size = query_base.shape[1]
    tok_count = layer_input.shape[0]
    full_input, full_gain, complete_down_factor = (
        lax.all_gather(layer_input, "tensor", axis=1, tiled=True),
        lax.all_gather(norm_gain, "tensor", axis=0, tiled=True),
        lax.all_gather(output_down_factor, "tensor", axis=0, tiled=True),
    )
    wide = full_input.astype(jnp.float32)
    scale = lax.rsqrt(jnp.mean(wide * wide, axis=1, keepdims=True) + 1e-05)
    normed = (wide * scale * full_gain.astype(jnp.float32)[None, :]).astype(jnp.bfloat16)
    local_normed = (
        layer_input.astype(jnp.float32) * scale * norm_gain.astype(jnp.float32)[None, :]
    ).astype(jnp.bfloat16)
    merged_query = (
        query_base.astype(jnp.float32)
        + 2.0 * jnp.dot(query_down, query_up, preferred_element_type=jnp.float32)
    ).astype(jnp.bfloat16)
    columns = normed
    query_raw = jnp.dot(
        columns,
        lax.all_gather(merged_query, ("engine", "fsdp"), axis=0, tiled=True),
        preferred_element_type=jnp.float32,
    )
    columns = local_normed
    kv_part = jnp.dot(
        columns,
        lax.all_gather(kv_base, ("engine", "fsdp"), axis=1, tiled=True)[0],
        preferred_element_type=jnp.float32,
    )
    kv_total = lax.psum(kv_part.astype(jnp.bfloat16), "tensor").astype(jnp.float32)
    places = positions[0]
    query = rotate(query_raw, places).astype(jnp.bfloat16)
    new_keys = rotate(kv_total[:, :head_size], places).astype(jnp.bfloat16)
    new_values = kv_total[:, head_size:].astype(jnp.bfloat16)
    head_out = attend(query, new_keys, new_values, cache_keys[0], cache_values[0], offsets[0])
    adapter_output_delta = jnp.einsum(
        "lz,zam->lam",
        complete_down_factor.astype(jnp.float32),
        output_up_factor.astype(jnp.float32),
    )
    combined_output_weight = (
        output_base_weight.astype(jnp.float32) + 2.0 * adapter_output_delta
    ).astype(jnp.bfloat16)
    own_rows = lax.all_to_all(
        combined_output_weight, "tensor", split_axis=0, concat_axis=1, tiled=True
    )
    terms = jnp.einsum(
        "tk,kbn->tbn",
        head_out,
        lax.all_gather(own_rows, ("engine", "fsdp"), axis=2, tiled=True),
        preferred_element_type=jnp.float32,
    )
    flat_terms = terms.reshape(tok_count, terms.shape[1] * terms.shape[2])
    attended = lax.psum_scatter(
        flat_terms.astype(jnp.bfloat16), "tensor", scatter_dimension=1, tiled=True
    )
    return attended


def kernel(
    n_f,
    input_ref,
    gain_ref,
    qbase_ref,
    qdown_ref,
    qup_ref,
    kvbase_ref,
    obase_ref,
    odown_ref,
    oup_ref,
    ckeys_ref,
    cvalues_ref,
    places_ref,
    offset_ref,
    result_ref,
    kv_buf,
    q_buf,
    o_buf,
    normed,
    squares,
    down_full,
    kv_part,
    q_total,
    heads,
    recv_sem,
    send_sem,
    y_recv,
    y_send,
    n_recv,
    n_send,
):
    engine = lax.axis_index("engine")
    z = lax.axis_index("fsdp")
    t = lax.axis_index("tensor")
    core = lax.rem(engine, 2)
    sibling = engine + 1 - 2 * core
    across = lax.rem(engine + 2, 4)
    other = 1 - t
    bufs = (kv_buf, q_buf, o_buf)
    groups = 4 * n_f
    tok = input_ref.shape[0]
    head = qbase_ref.shape[1]
    piece = kvbase_ref.shape[0]
    half_groups = groups // 2
    rank = odown_ref.shape[1]
    width = 2 * input_ref.shape[1]

    def copy(m, g, way):
        target = {
            SIB: (sibling, z, t),
            CROSS: (across, z, t),
            LEFT: (engine, jnp.maximum(z - 1, 0), t),
            RIGHT: (engine, jnp.minimum(z + 1, n_f - 1), t),
        }[way]
        return pltpu.make_async_remote_copy(
            src_ref=bufs[m].at[g],
            dst_ref=bufs[m].at[g],
            send_sem=send_sem.at[m, way, g],
            recv_sem=recv_sem.at[m, g],
            device_id=target,
            device_id_type=MESH,
        )

    def to_partner(ref, k):
        return pltpu.make_async_remote_copy(
            src_ref=ref.at[t],
            dst_ref=ref.at[t],
            send_sem=y_send.at[k],
            recv_sem=y_recv.at[k],
            device_id=(engine, z, other),
            device_id_type=MESH,
        )

    def from_partner(ref, k):
        return pltpu.make_async_remote_copy(
            src_ref=ref.at[other],
            dst_ref=ref.at[other],
            send_sem=y_send.at[k],
            recv_sem=y_recv.at[k],
            device_id=(engine, z, other),
            device_id_type=MESH,
        )

    def normed_copy(side, k):
        rows = normed.at[pl.ds(side * groups + 2 * k, 2)]
        return pltpu.make_async_remote_copy(
            src_ref=rows,
            dst_ref=rows,
            send_sem=n_send.at[k],
            recv_sem=n_recv.at[k],
            device_id=(engine, z, other),
            device_id_type=MESH,
        )

    def own(m):
        g = engine * n_f + z
        copy(m, g, CROSS).start()

        @pl.when(z > 0)
        def _():
            copy(m, g, LEFT).start()

        @pl.when(z < n_f - 1)
        def _():
            copy(m, g, RIGHT).start()

        copy(m, g, SIB).start()

    def along(m, d):
        @pl.when(z >= d)
        def _():
            g = engine * n_f + z - d
            copy(m, g, SIB).wait_recv()

            @pl.when(z < n_f - 1)
            def _():
                copy(m, g, RIGHT).start()

            copy(m, g, CROSS).start()
            copy(m, g, SIB).start()

        @pl.when(z + d < n_f)
        def _():
            g = engine * n_f + z + d
            copy(m, g, SIB).wait_recv()

            @pl.when(z > 0)
            def _():
                copy(m, g, LEFT).start()

            copy(m, g, CROSS).start()
            copy(m, g, SIB).start()

    def crossing(m, d):
        def take(zz):
            g = across * n_f + zz
            copy(m, g, SIB).wait_recv()
            copy(m, g, SIB).start()

        if d == 0:
            take(z)
        else:
            pl.when(z >= d)(lambda: take(z - d))
            pl.when(z + d < n_f)(lambda: take(z + d))

    def from_sibling(m):
        def both(k, carry):
            copy(m, sibling * n_f + k, SIB).wait_recv()
            copy(m, lax.rem(sibling + 2, 4) * n_f + k, SIB).wait_recv()
            return carry

        lax.fori_loop(0, n_f, both, 0)

    barrier = pltpu.get_barrier_semaphore()

    def greet(target):
        pl.semaphore_signal(barrier, inc=1, device_id=target, device_id_type=MESH)

    greet((sibling, z, t))
    greet((across, z, t))
    greet((engine, z, other))
    pl.when(z > 0)(lambda: greet((engine, z - 1, t)))
    pl.when(z < n_f - 1)(lambda: greet((engine, z + 1, t)))

    mine = engine * n_f + z
    kv_buf[mine] = kvbase_ref[...]
    total = jnp.zeros((tok, 128), jnp.float32)
    for k in range(input_ref.shape[1] // 128):
        wide = input_ref[:, k * 128 : (k + 1) * 128].astype(jnp.float32)
        total = total + wide * wide
    squares[t] = total
    down_full[t] = jnp.zeros(down_full.shape[1:], jnp.bfloat16)
    down_full[t, :, :rank] = odown_ref[...]

    pl.semaphore_wait(barrier, 5 - (z == 0).astype(jnp.int32) - (z == n_f - 1).astype(jnp.int32))

    own(KV)
    to_partner(squares, 0).start()
    to_partner(down_full, 1).start()
    q_buf[mine] = (
        qbase_ref[...].astype(jnp.float32)
        + 2.0 * jnp.dot(qdown_ref[...], qup_ref[...], preferred_element_type=jnp.float32)
    ).astype(jnp.bfloat16)

    from_partner(squares, 0).wait_recv()
    mean = jnp.sum(squares[0] + squares[1], axis=1, keepdims=True) * (1.0 / width)
    scale = lax.rsqrt(mean + 1e-05)
    for k in range(groups):
        cut = slice(k * piece, (k + 1) * piece)
        normed[t * groups + k] = (
            input_ref[:, cut].astype(jnp.float32) * scale * gain_ref[:, cut].astype(jnp.float32)
        ).astype(jnp.bfloat16)
        if k % 2 == 1:
            normed_copy(t, k // 2).start()

    along(KV, 1)
    own(QUERY)
    crossing(KV, 0)
    along(KV, 2)

    from_partner(down_full, 1).wait_recv()
    for side in range(2):
        rows = slice(side * head, (side + 1) * head)
        o_buf[mine, rows, :] = (
            obase_ref[rows, :].astype(jnp.float32)
            + 2.0
            * jnp.dot(
                down_full[side, :, :rank], oup_ref[...], preferred_element_type=jnp.float32
            )
        ).astype(jnp.bfloat16)

    crossing(KV, 1)
    along(KV, 3)
    crossing(KV, 2)
    along(QUERY, 1)
    crossing(KV, 3)
    own(OUT)
    crossing(QUERY, 0)
    along(QUERY, 2)

    from_sibling(KV)
    kv_part[t] = jnp.zeros(kv_part.shape[1:], jnp.float32)

    def kv_step(g, carry):
        kv_part[t] += jnp.dot(
            normed[t * groups + g], kv_buf[g], preferred_element_type=jnp.float32
        )
        return carry

    lax.fori_loop(0, groups // 2, kv_step, 0)
    crossing(QUERY, 1)
    along(QUERY, 3)
    lax.fori_loop(groups // 2, groups, kv_step, 0)
    to_partner(kv_part, 2).start()
    along(OUT, 1)
    crossing(QUERY, 2)
    crossing(QUERY, 3)

    lane = lax.broadcasted_iota(jnp.int32, (tok, head), 1)
    low = lane < head // 2
    index = jnp.where(low, lane, lane - head // 2).astype(jnp.float32)
    inverse = jnp.exp(index * (-2.0 / head) * jnp.log(jnp.full((tok, head), 500000.0, jnp.float32)))
    places = jnp.broadcast_to(places_ref[...].astype(jnp.float32), (head, tok)).T
    angle = places * inverse
    cosine = jnp.cos(angle)
    sine = jnp.where(low, -jnp.sin(angle), jnp.sin(angle))

    def rope(values):
        return values * cosine + pltpu.roll(values, head // 2, 1) * sine

    from_sibling(QUERY)
    q_total[...] = jnp.zeros_like(q_total)

    def q_step(g):
        q_total[...] += jnp.dot(
            normed[2 * g], q_buf[g, :piece, :], preferred_element_type=jnp.float32
        ) + jnp.dot(normed[2 * g + 1], q_buf[g, piece:, :], preferred_element_type=jnp.float32)

    def q_near(k, carry):
        q_step(t * half_groups + k)
        return carry

    def q_far(k, carry):
        normed_copy(other, k).wait_recv()
        q_step(other * half_groups + k)
        return carry

    lax.fori_loop(0, half_groups, q_near, 0)
    crossing(OUT, 0)
    along(OUT, 2)
    lax.fori_loop(0, half_groups, q_far, 0)

    query = rope(q_total[...]).astype(jnp.bfloat16)
    from_partner(kv_part, 2).wait_recv()
    kv = kv_part[0] + kv_part[1]
    new_keys = rope(kv[:, :head]).astype(jnp.bfloat16)
    new_values = kv[:, head:].astype(jnp.bfloat16)
    dims = (((1,), (1,)), ((), ()))
    slots = ckeys_ref.shape[0]
    factor = head ** (-0.5)
    old = lax.dot_general(query, ckeys_ref[...], dims, preferred_element_type=jnp.float32) * factor
    new = lax.dot_general(query, new_keys, dims, preferred_element_type=jnp.float32) * factor
    seen = lax.broadcasted_iota(jnp.int32, (tok, slots), 1) < offset_ref[0]
    rows = lax.broadcasted_iota(jnp.int32, (tok, tok), 0)
    columns = lax.broadcasted_iota(jnp.int32, (tok, tok), 1)
    old = jnp.where(seen, old, jnp.float32(-1e30))
    new = jnp.where(columns <= rows, new, jnp.float32(-1e30))
    top = jnp.maximum(
        jnp.max(old, axis=1, keepdims=True), jnp.max(new, axis=1, keepdims=True)
    )
    old = jnp.exp(old - top)
    new = jnp.exp(new - top)
    summed = jnp.sum(old, axis=1, keepdims=True) + jnp.sum(new, axis=1, keepdims=True)
    old = (old / summed).astype(jnp.bfloat16)
    new = (new / summed).astype(jnp.bfloat16)
    heads[t] = (
        jnp.dot(old, cvalues_ref[...], preferred_element_type=jnp.float32)
        + jnp.dot(new, new_values, preferred_element_type=jnp.float32)
    ).astype(jnp.bfloat16)
    to_partner(heads, 3).start()
    along(OUT, 3)
    from_partner(heads, 3).wait_recv()

    def project(g):
        first = jnp.dot(heads[0], o_buf[g, :head, :], preferred_element_type=jnp.float32)
        second = jnp.dot(heads[1], o_buf[g, head:, :], preferred_element_type=jnp.float32)
        both = first.astype(jnp.bfloat16).astype(jnp.float32) + second.astype(
            jnp.bfloat16
        ).astype(jnp.float32)
        result_ref[:, pl.ds(pl.multiple_of(g * piece, piece), piece)] = both.astype(jnp.bfloat16)

    def column(which):
        def step(k, carry):
            project(which * n_f + k)
            return carry

        lax.fori_loop(0, n_f, step, 0)

    crossing(OUT, 1)
    column(engine)
    crossing(OUT, 2)
    crossing(OUT, 3)
    column(across)

    def sibling_column(which):
        def step(k, carry):
            g = which * n_f + k
            copy(OUT, g, SIB).wait_recv()
            project(g)
            return carry

        lax.fori_loop(0, n_f, step, 0)

    sibling_column(sibling)
    sibling_column(lax.rem(sibling + 2, 4))

    for m in range(3):

        def drain(k, carry, m=m):
            g = engine * n_f + k
            copy(m, g, SIB).wait_send()
            copy(m, g, CROSS).wait_send()
            copy(m, across * n_f + k, SIB).wait_send()

            @pl.when((z > 0) & (k >= z))
            def _():
                copy(m, g, LEFT).wait_send()

            @pl.when((z < n_f - 1) & (k <= z))
            def _():
                copy(m, g, RIGHT).wait_send()

            return carry

        lax.fori_loop(0, n_f, drain, 0)

    def drain_normed(k, carry):
        normed_copy(t, k).wait_send()
        return carry

    lax.fori_loop(0, half_groups, drain_normed, 0)
    to_partner(squares, 0).wait_send()
    to_partner(down_full, 1).wait_send()
    to_partner(kv_part, 2).wait_send()
    to_partner(heads, 3).wait_send()


def per_device(
    n_f,
    layer_input,
    norm_gain,
    query_base,
    query_down,
    query_up,
    kv_base,
    output_base_weight,
    output_down_factor,
    output_up_factor,
    cache_keys,
    cache_values,
    positions,
    offsets,
):
    tok, features = layer_input.shape
    depth, head = query_base.shape
    groups = 4 * n_f
    kv_base = kv_base[0]
    output_base_weight = output_base_weight[:, 0]
    output_up_factor = output_up_factor[:, 0]
    piece = kv_base.shape[0]
    vmem = pl.BlockSpec(memory_space=pltpu.VMEM)
    smem = pl.BlockSpec(memory_space=pltpu.SMEM)
    dma = pltpu.SemaphoreType.DMA
    return pl.pallas_call(
        functools.partial(kernel, n_f),
        out_shape=jax.ShapeDtypeStruct((tok, features), jnp.bfloat16),
        in_specs=[vmem] * 12 + [smem],
        out_specs=vmem,
        scratch_shapes=[
            pltpu.VMEM((groups,) + kv_base.shape, jnp.bfloat16),
            pltpu.VMEM((groups,) + query_base.shape, jnp.bfloat16),
            pltpu.VMEM((groups,) + output_base_weight.shape, jnp.bfloat16),
            pltpu.VMEM((2 * groups, tok, piece), jnp.bfloat16),
            pltpu.VMEM((2, tok, 128), jnp.float32),
            pltpu.VMEM((2, head, 128), jnp.bfloat16),
            pltpu.VMEM((2, tok, 2 * head), jnp.float32),
            pltpu.VMEM((tok, head), jnp.float32),
            pltpu.VMEM((2, tok, head), jnp.bfloat16),
            dma((3, groups)),
            dma((3, 4, groups)),
            dma((4,)),
            dma((4,)),
            dma((groups // 2,)),
            dma((groups // 2,)),
        ],
        compiler_params=pltpu.CompilerParams(
            collective_id=0, has_side_effects=True, vmem_limit_bytes=48 * 1024 * 1024
        ),
    )(
        layer_input,
        norm_gain[None, :],
        query_base,
        query_down,
        query_up,
        kv_base,
        output_base_weight,
        output_down_factor,
        output_up_factor,
        cache_keys[0],
        cache_values[0],
        positions,
        offsets,
    )


def solution(mesh):
    in_specs = (
        P(("engine", "fsdp"), "tensor"),
        P("tensor"),
        P(("engine", "fsdp"), "tensor"),
        P(("engine", "fsdp"), None),
        P(None, "tensor"),
        P("tensor", ("engine", "fsdp"), None),
        P(None, "tensor", ("engine", "fsdp")),
        P("tensor", None),
        P(None, "tensor", ("engine", "fsdp")),
        P(("engine", "fsdp"), None, None),
        P(("engine", "fsdp"), None, None),
        P(("engine", "fsdp"), None),
        P(("engine", "fsdp")),
    )
    out_specs = P(("engine", "fsdp"), "tensor")
    shape = dict(mesh.shape)
    paired = shape["tensor"] == 2 and shape["engine"] == 4
    body = functools.partial(per_device, shape["fsdp"]) if paired else per_device_plain
    return jax.shard_map(
        body, mesh=mesh, in_specs=in_specs, out_specs=out_specs, check_vma=False
    )
```

```python
import functools

import jax
import jax.numpy as jnp
from jax import lax
from jax.experimental import pallas as pl
from jax.experimental.pallas import tpu as pltpu
from jax.sharding import PartitionSpec as P

MESH = pl.DeviceIdType.MESH
KV, QUERY, OUT = 0, 1, 2
SIB, CROSS, LEFT, RIGHT = 0, 1, 2, 3


def rotate(values, places):
    half = values.shape[-1] // 2
    index = jnp.arange(half).astype(jnp.float32)
    inverse = jnp.exp(index * (-2.0 / values.shape[-1]) * jnp.log(jnp.float32(500000.0)))
    angle = places.astype(jnp.float32)[:, None] * inverse[None, :]
    cosine = jnp.cos(angle)
    sine = jnp.sin(angle)
    first = values[:, :half]
    second = values[:, half:]
    return jnp.concatenate([first * cosine - second * sine, second * cosine + first * sine], axis=1)


def attend(query, new_keys, new_values, old_keys, old_values, offset):
    tok_count = query.shape[0]
    slots = old_keys.shape[0]
    keys_all = jnp.concatenate([old_keys, new_keys], axis=0)
    values_all = jnp.concatenate([old_values, new_values], axis=0)
    scores = jnp.dot(query, keys_all.T, preferred_element_type=jnp.float32) * query.shape[-1] ** (
        -0.5
    )
    slot_seen = jnp.broadcast_to(jnp.arange(slots)[None, :] < offset, (tok_count, slots))
    rows = jnp.arange(tok_count)
    new_seen = rows[None, :] <= rows[:, None]
    seen = jnp.concatenate([slot_seen, new_seen], axis=1)
    scores = jnp.where(seen, scores, jnp.float32(-1e30))
    top = jnp.max(scores, axis=1, keepdims=True)
    probs = jnp.exp(scores - top)
    weights = (probs / jnp.sum(probs, axis=1, keepdims=True)).astype(jnp.bfloat16)
    return jnp.dot(weights, values_all, preferred_element_type=jnp.float32).astype(jnp.bfloat16)


def per_device_plain(
    layer_input,
    norm_gain,
    query_base,
    query_down,
    query_up,
    kv_base,
    output_base_weight,
    output_down_factor,
    output_up_factor,
    cache_keys,
    cache_values,
    positions,
    offsets,
):
    head_size = query_base.shape[1]
    tok_count = layer_input.shape[0]
    full_input, full_gain, complete_down_factor = (
        lax.all_gather(layer_input, "tensor", axis=1, tiled=True),
        lax.all_gather(norm_gain, "tensor", axis=0, tiled=True),
        lax.all_gather(output_down_factor, "tensor", axis=0, tiled=True),
    )
    wide = full_input.astype(jnp.float32)
    scale = lax.rsqrt(jnp.mean(wide * wide, axis=1, keepdims=True) + 1e-05)
    normed = (wide * scale * full_gain.astype(jnp.float32)[None, :]).astype(jnp.bfloat16)
    local_normed = (
        layer_input.astype(jnp.float32) * scale * norm_gain.astype(jnp.float32)[None, :]
    ).astype(jnp.bfloat16)
    merged_query = (
        query_base.astype(jnp.float32)
        + 2.0 * jnp.dot(query_down, query_up, preferred_element_type=jnp.float32)
    ).astype(jnp.bfloat16)
    columns = normed
    query_raw = jnp.dot(
        columns,
        lax.all_gather(merged_query, ("engine", "fsdp"), axis=0, tiled=True),
        preferred_element_type=jnp.float32,
    )
    columns = local_normed
    kv_part = jnp.dot(
        columns,
        lax.all_gather(kv_base, ("engine", "fsdp"), axis=1, tiled=True)[0],
        preferred_element_type=jnp.float32,
    )
    kv_total = lax.psum(kv_part.astype(jnp.bfloat16), "tensor").astype(jnp.float32)
    places = positions[0]
    query = rotate(query_raw, places).astype(jnp.bfloat16)
    new_keys = rotate(kv_total[:, :head_size], places).astype(jnp.bfloat16)
    new_values = kv_total[:, head_size:].astype(jnp.bfloat16)
    head_out = attend(query, new_keys, new_values, cache_keys[0], cache_values[0], offsets[0])
    adapter_output_delta = jnp.einsum(
        "lz,zam->lam",
        complete_down_factor.astype(jnp.float32),
        output_up_factor.astype(jnp.float32),
    )
    combined_output_weight = (
        output_base_weight.astype(jnp.float32) + 2.0 * adapter_output_delta
    ).astype(jnp.bfloat16)
    own_rows = lax.all_to_all(
        combined_output_weight, "tensor", split_axis=0, concat_axis=1, tiled=True
    )
    terms = jnp.einsum(
        "tk,kbn->tbn",
        head_out,
        lax.all_gather(own_rows, ("engine", "fsdp"), axis=2, tiled=True),
        preferred_element_type=jnp.float32,
    )
    flat_terms = terms.reshape(tok_count, terms.shape[1] * terms.shape[2])
    attended = lax.psum_scatter(
        flat_terms.astype(jnp.bfloat16), "tensor", scatter_dimension=1, tiled=True
    )
    return attended


def kernel(
    n_f,
    input_hbm,
    gain_hbm,
    qbase_hbm,
    qdown_hbm,
    qup_hbm,
    kvbase_hbm,
    obase_hbm,
    odown_hbm,
    oup_hbm,
    ckeys_hbm,
    cvalues_hbm,
    places_hbm,
    offset_ref,
    result_ref,
    input_ref,
    gain_ref,
    qbase_ref,
    qdown_ref,
    qup_ref,
    obase_ref,
    odown_ref,
    oup_ref,
    ckeys_ref,
    cvalues_ref,
    places_ref,
    kv_buf,
    q_buf,
    o_buf,
    normed,
    squares,
    down_full,
    kv_part,
    q_total,
    heads,
    cosine_ref,
    sine_ref,
    recv_sem,
    send_sem,
    y_recv,
    y_send,
    n_recv,
    n_send,
    load_sem,
):
    engine = lax.axis_index("engine")
    z = lax.axis_index("fsdp")
    t = lax.axis_index("tensor")
    core = lax.rem(engine, 2)
    sibling = engine + 1 - 2 * core
    across = lax.rem(engine + 2, 4)
    other = 1 - t
    bufs = (kv_buf, q_buf, o_buf)
    groups = 4 * n_f
    tok = input_ref.shape[0]
    head = qbase_ref.shape[1]
    piece = kvbase_hbm.shape[0]
    half_groups = groups // 2
    mine = engine * n_f + z
    width = 2 * input_ref.shape[1]

    def copy(m, g, way):
        target = {
            SIB: (sibling, z, t),
            CROSS: (across, z, t),
            LEFT: (engine, jnp.maximum(z - 1, 0), t),
            RIGHT: (engine, jnp.minimum(z + 1, n_f - 1), t),
        }[way]
        return pltpu.make_async_remote_copy(
            src_ref=bufs[m].at[g],
            dst_ref=bufs[m].at[g],
            send_sem=send_sem.at[m, way, g],
            recv_sem=recv_sem.at[m, g],
            device_id=target,
            device_id_type=MESH,
        )

    def to_partner(ref, k):
        return pltpu.make_async_remote_copy(
            src_ref=ref.at[t],
            dst_ref=ref.at[t],
            send_sem=y_send.at[k],
            recv_sem=y_recv.at[k],
            device_id=(engine, z, other),
            device_id_type=MESH,
        )

    def from_partner(ref, k):
        return pltpu.make_async_remote_copy(
            src_ref=ref.at[other],
            dst_ref=ref.at[other],
            send_sem=y_send.at[k],
            recv_sem=y_recv.at[k],
            device_id=(engine, z, other),
            device_id_type=MESH,
        )

    def normed_copy(side, k):
        rows = normed.at[pl.ds(side * groups + 2 * k, 2)]
        return pltpu.make_async_remote_copy(
            src_ref=rows,
            dst_ref=rows,
            send_sem=n_send.at[k],
            recv_sem=n_recv.at[k],
            device_id=(engine, z, other),
            device_id_type=MESH,
        )

    def own(m):
        g = engine * n_f + z
        copy(m, g, CROSS).start()

        @pl.when(z > 0)
        def _():
            copy(m, g, LEFT).start()

        @pl.when(z < n_f - 1)
        def _():
            copy(m, g, RIGHT).start()

        copy(m, g, SIB).start()

    early = (n_f // 2 - 1, n_f // 2)

    def relay_cross(m, g, zz):
        if m == QUERY:
            pl.when((zz != early[0]) & (zz != early[1]))(lambda: copy(m, g, CROSS).start())
        else:
            copy(m, g, CROSS).start()

    def along(m, d):
        @pl.when(z >= d)
        def _():
            g = engine * n_f + z - d
            copy(m, g, SIB).wait_recv()

            @pl.when(z < n_f - 1)
            def _():
                copy(m, g, RIGHT).start()

            relay_cross(m, g, z - d)
            copy(m, g, SIB).start()

        @pl.when(z + d < n_f)
        def _():
            g = engine * n_f + z + d
            copy(m, g, SIB).wait_recv()

            @pl.when(z > 0)
            def _():
                copy(m, g, LEFT).start()

            relay_cross(m, g, z + d)
            copy(m, g, SIB).start()

    def crossing(m, d):
        def take(zz):
            g = across * n_f + zz
            copy(m, g, SIB).wait_recv()
            copy(m, g, SIB).start()

        def late(zz):
            return (zz != early[0]) & (zz != early[1]) if m == QUERY else zz >= 0

        if d == 0:
            take(z)
            if m == QUERY:
                g = across * n_f + z

                @pl.when(((z == early[0]) | (z == early[1])) & (z > 0))
                def _():
                    copy(m, g, LEFT).start()

                @pl.when(((z == early[0]) | (z == early[1])) & (z < n_f - 1))
                def _():
                    copy(m, g, RIGHT).start()

        else:
            pl.when((z >= d) & late(z - d))(lambda: take(z - d))
            pl.when((z + d < n_f) & late(z + d))(lambda: take(z + d))

    def far(m):
        for zz in early:
            g = across * n_f + zz

            @pl.when(z != zz)
            def _(g=g, zz=zz):
                copy(m, g, SIB).wait_recv()
                copy(m, g, SIB).start()

                @pl.when((z < zz) & (z > 0))
                def _():
                    copy(m, g, LEFT).start()

                @pl.when((z > zz) & (z < n_f - 1))
                def _():
                    copy(m, g, RIGHT).start()

    def from_sibling(m):
        def both(k, carry):
            copy(m, sibling * n_f + k, SIB).wait_recv()
            copy(m, lax.rem(sibling + 2, 4) * n_f + k, SIB).wait_recv()
            return carry

        lax.fori_loop(0, n_f, both, 0)

    loads = [
        pltpu.make_async_copy(source, target, load_sem.at[k])
        for k, (source, target) in enumerate(
            (
                (kvbase_hbm, kv_buf.at[mine]),
                (odown_hbm, odown_ref),
                (input_hbm, input_ref),
                (qbase_hbm, qbase_ref),
                (qdown_hbm, qdown_ref),
                (qup_hbm, qup_ref),
                (gain_hbm, gain_ref),
                (obase_hbm, obase_ref),
                (oup_hbm, oup_ref),
                (places_hbm, places_ref),
                (ckeys_hbm, ckeys_ref),
                (cvalues_hbm, cvalues_ref),
            )
        )
    ]
    for load in loads:
        load.start()

    barrier = pltpu.get_barrier_semaphore()

    def greet(target):
        pl.semaphore_signal(barrier, inc=1, device_id=target, device_id_type=MESH)

    greet((sibling, z, t))
    greet((across, z, t))
    greet((engine, z, other))
    pl.when(z > 0)(lambda: greet((engine, z - 1, t)))
    pl.when(z < n_f - 1)(lambda: greet((engine, z + 1, t)))

    loads[0].wait()
    loads[1].wait()
    down_full[t] = odown_ref[...]
    pl.semaphore_wait(barrier, 5 - (z == 0).astype(jnp.int32) - (z == n_f - 1).astype(jnp.int32))

    own(KV)
    to_partner(down_full, 1).start()
    loads[2].wait()
    total = jnp.zeros((tok, 128), jnp.float32)
    for k in range(input_ref.shape[1] // 128):
        wide = input_ref[:, k * 128 : (k + 1) * 128].astype(jnp.float32)
        total = total + wide * wide
    squares[t] = total
    to_partner(squares, 0).start()

    over_rank = (((0,), (0,)), ((), ()))
    for k in range(3, 6):
        loads[k].wait()
    q_buf[mine] = (
        qbase_ref[...].astype(jnp.float32)
        + 2.0
        * lax.dot_general(
            qdown_ref[...], qup_ref[...], over_rank, preferred_element_type=jnp.float32
        )
    ).astype(jnp.bfloat16)
    own(QUERY)

    loads[6].wait()
    from_partner(squares, 0).wait_recv()
    mean = jnp.sum(squares[0] + squares[1], axis=1, keepdims=True) * (1.0 / width)
    scale = jnp.broadcast_to(lax.rsqrt(mean + 1e-05), (tok, 128))
    each = piece // 128
    for k in range(groups):
        for part in range(each):
            at = k * each + part
            normed[t * groups + k, :, part * 128 : (part + 1) * 128] = (
                input_ref[:, at * 128 : (at + 1) * 128].astype(jnp.float32)
                * scale
                * gain_ref[at : at + 1, :].astype(jnp.float32)
            ).astype(jnp.bfloat16)
        if k % 2 == 1:
            normed_copy(t, k // 2).start()

    for k in range(7, len(loads)):
        loads[k].wait()

    along(KV, 1)
    crossing(KV, 0)
    along(KV, 2)

    from_partner(down_full, 1).wait_recv()
    for side in range(2):
        rows = slice(side * head, (side + 1) * head)
        o_buf[mine, rows, :] = (
            obase_ref[rows, :].astype(jnp.float32)
            + 2.0
            * lax.dot_general(
                down_full[side], oup_ref[...], over_rank, preferred_element_type=jnp.float32
            )
        ).astype(jnp.bfloat16)
    own(OUT)

    along(QUERY, 1)
    crossing(KV, 1)
    along(KV, 3)
    crossing(QUERY, 0)
    crossing(KV, 2)

    lane = lax.broadcasted_iota(jnp.int32, (tok, head), 1)
    low = lane < head // 2
    index = jnp.where(low, lane, lane - head // 2).astype(jnp.float32)
    inverse = jnp.exp(index * (-2.0 / head) * jnp.log(jnp.full((tok, head), 500000.0, jnp.float32)))
    places = jnp.broadcast_to(places_ref[...].astype(jnp.float32), (head, tok)).T
    angle = places * inverse
    cosine_ref[...] = jnp.cos(angle)
    sine_ref[...] = jnp.where(low, -jnp.sin(angle), jnp.sin(angle))

    def rope(values):
        return values * cosine_ref[...] + pltpu.roll(values, head // 2, 1) * sine_ref[...]

    along(QUERY, 2)
    far(QUERY)
    crossing(KV, 3)
    from_sibling(KV)
    kv_part[t] = jnp.zeros(kv_part.shape[1:], jnp.float32)

    def kv_step(g, carry):
        kv_part[t] += jnp.dot(
            normed[t * groups + g], kv_buf[g], preferred_element_type=jnp.float32
        )
        return carry

    lax.fori_loop(0, groups // 2, kv_step, 0)
    along(QUERY, 3)
    crossing(QUERY, 1)
    along(OUT, 1)
    lax.fori_loop(groups // 2, groups, kv_step, 0)
    to_partner(kv_part, 2).start()
    along(OUT, 2)
    crossing(QUERY, 2)
    crossing(QUERY, 3)
    crossing(OUT, 0)

    from_sibling(QUERY)
    q_total[...] = jnp.zeros_like(q_total)

    def q_step(g):
        q_total[...] += jnp.dot(
            normed[2 * g], q_buf[g, :piece, :], preferred_element_type=jnp.float32
        ) + jnp.dot(normed[2 * g + 1], q_buf[g, piece:, :], preferred_element_type=jnp.float32)

    def q_near(k, carry):
        q_step(t * half_groups + k)
        return carry

    def q_far(k, carry):
        normed_copy(other, k).wait_recv()
        q_step(other * half_groups + k)
        return carry

    lax.fori_loop(0, half_groups, q_near, 0)
    along(OUT, 3)
    crossing(OUT, 1)
    lax.fori_loop(0, half_groups, q_far, 0)

    query = rope(q_total[...]).astype(jnp.bfloat16)
    from_partner(kv_part, 2).wait_recv()
    kv = kv_part[0] + kv_part[1]
    new_keys = rope(kv[:, :head]).astype(jnp.bfloat16)
    new_values = kv[:, head:].astype(jnp.bfloat16)
    dims = (((1,), (1,)), ((), ()))
    slots = ckeys_ref.shape[0]
    factor = head ** (-0.5)
    old = lax.dot_general(query, ckeys_ref[...], dims, preferred_element_type=jnp.float32) * factor
    new = lax.dot_general(query, new_keys, dims, preferred_element_type=jnp.float32) * factor
    seen = lax.broadcasted_iota(jnp.int32, (tok, slots), 1) < offset_ref[0]
    rows = lax.broadcasted_iota(jnp.int32, (tok, tok), 0)
    columns = lax.broadcasted_iota(jnp.int32, (tok, tok), 1)
    old = jnp.where(seen, old, jnp.float32(-1e30))
    new = jnp.where(columns <= rows, new, jnp.float32(-1e30))
    top = jnp.maximum(
        jnp.max(old, axis=1, keepdims=True), jnp.max(new, axis=1, keepdims=True)
    )
    old = jnp.exp(old - top)
    new = jnp.exp(new - top)
    summed = jnp.sum(old, axis=1, keepdims=True) + jnp.sum(new, axis=1, keepdims=True)
    old = (old / summed).astype(jnp.bfloat16)
    new = (new / summed).astype(jnp.bfloat16)
    heads[t] = (
        jnp.dot(old, cvalues_ref[...], preferred_element_type=jnp.float32)
        + jnp.dot(new, new_values, preferred_element_type=jnp.float32)
    ).astype(jnp.bfloat16)
    to_partner(heads, 3).start()
    from_partner(heads, 3).wait_recv()

    def project(g):
        first = jnp.dot(heads[0], o_buf[g, :head, :], preferred_element_type=jnp.float32)
        second = jnp.dot(heads[1], o_buf[g, head:, :], preferred_element_type=jnp.float32)
        both = first.astype(jnp.bfloat16).astype(jnp.float32) + second.astype(
            jnp.bfloat16
        ).astype(jnp.float32)
        result_ref[:, pl.ds(pl.multiple_of(g * piece, piece), piece)] = both.astype(jnp.bfloat16)

    def column(which):
        def step(k, carry):
            project(which * n_f + k)
            return carry

        lax.fori_loop(0, n_f, step, 0)

    column(engine)
    crossing(OUT, 2)
    crossing(OUT, 3)
    column(across)

    def sibling_column(which):
        def step(k, carry):
            g = which * n_f + k
            copy(OUT, g, SIB).wait_recv()
            project(g)
            return carry

        lax.fori_loop(0, n_f, step, 0)

    sibling_column(sibling)
    sibling_column(lax.rem(sibling + 2, 4))

    for m in range(3):

        def drain(k, carry, m=m):
            g = engine * n_f + k
            copy(m, g, SIB).wait_send()
            far_g = across * n_f + k
            copy(m, far_g, SIB).wait_send()
            first = (k == early[0]) | (k == early[1])
            if m == QUERY:
                pl.when(~first | (k == z))(lambda: copy(m, g, CROSS).wait_send())

                @pl.when(first & (z > 0) & (k >= z))
                def _():
                    copy(m, far_g, LEFT).wait_send()

                @pl.when(first & (z < n_f - 1) & (k <= z))
                def _():
                    copy(m, far_g, RIGHT).wait_send()

            else:
                copy(m, g, CROSS).wait_send()

            @pl.when((z > 0) & (k >= z))
            def _():
                copy(m, g, LEFT).wait_send()

            @pl.when((z < n_f - 1) & (k <= z))
            def _():
                copy(m, g, RIGHT).wait_send()

            return carry

        lax.fori_loop(0, n_f, drain, 0)

    def drain_normed(k, carry):
        normed_copy(t, k).wait_send()
        return carry

    lax.fori_loop(0, half_groups, drain_normed, 0)
    to_partner(squares, 0).wait_send()
    to_partner(down_full, 1).wait_send()
    to_partner(kv_part, 2).wait_send()
    to_partner(heads, 3).wait_send()


def per_device(
    n_f,
    layer_input,
    norm_gain,
    query_base,
    query_down,
    query_up,
    kv_base,
    output_base_weight,
    output_down_factor,
    output_up_factor,
    cache_keys,
    cache_values,
    positions,
    offsets,
):
    tok, features = layer_input.shape
    depth, head = query_base.shape
    rank = query_up.shape[0]
    groups = 4 * n_f
    kv_base = kv_base[0]
    output_base_weight = output_base_weight[:, 0]
    output_up_factor = output_up_factor[:, 0]
    piece = kv_base.shape[0]
    vmem = pl.BlockSpec(memory_space=pltpu.VMEM)
    hbm = pl.BlockSpec(memory_space=pltpu.HBM)
    smem = pl.BlockSpec(memory_space=pltpu.SMEM)
    dma = pltpu.SemaphoreType.DMA
    return pl.pallas_call(
        functools.partial(kernel, n_f),
        out_shape=jax.ShapeDtypeStruct((tok, features), jnp.bfloat16),
        in_specs=[hbm] * 12 + [smem],
        out_specs=vmem,
        scratch_shapes=[
            pltpu.VMEM((tok, features), jnp.bfloat16),
            pltpu.VMEM((features // 128, 128), jnp.bfloat16),
            pltpu.VMEM(query_base.shape, jnp.bfloat16),
            pltpu.VMEM((rank, depth), jnp.bfloat16),
            pltpu.VMEM(query_up.shape, jnp.bfloat16),
            pltpu.VMEM(output_base_weight.shape, jnp.bfloat16),
            pltpu.VMEM((rank, head), jnp.bfloat16),
            pltpu.VMEM(output_up_factor.shape, jnp.bfloat16),
            pltpu.VMEM(cache_keys.shape[1:], jnp.bfloat16),
            pltpu.VMEM(cache_values.shape[1:], jnp.bfloat16),
            pltpu.VMEM(positions.shape, jnp.int32),
            pltpu.VMEM((groups,) + kv_base.shape, jnp.bfloat16),
            pltpu.VMEM((groups,) + query_base.shape, jnp.bfloat16),
            pltpu.VMEM((groups,) + output_base_weight.shape, jnp.bfloat16),
            pltpu.VMEM((2 * groups, tok, piece), jnp.bfloat16),
            pltpu.VMEM((2, tok, 128), jnp.float32),
            pltpu.VMEM((2, rank, head), jnp.bfloat16),
            pltpu.VMEM((2, tok, 2 * head), jnp.float32),
            pltpu.VMEM((tok, head), jnp.float32),
            pltpu.VMEM((2, tok, head), jnp.bfloat16),
            pltpu.VMEM((tok, head), jnp.float32),
            pltpu.VMEM((tok, head), jnp.float32),
            dma((3, groups)),
            dma((3, 4, groups)),
            dma((4,)),
            dma((4,)),
            dma((groups // 2,)),
            dma((groups // 2,)),
            dma((12,)),
        ],
        compiler_params=pltpu.CompilerParams(
            collective_id=0, has_side_effects=True, vmem_limit_bytes=48 * 1024 * 1024
        ),
    )(
        layer_input,
        norm_gain.reshape(-1, 128),
        query_base,
        query_down.T,
        query_up,
        kv_base,
        output_base_weight,
        output_down_factor.T,
        output_up_factor,
        cache_keys[0],
        cache_values[0],
        positions,
        offsets,
    )


def solution(mesh):
    in_specs = (
        P(("engine", "fsdp"), "tensor"),
        P("tensor"),
        P(("engine", "fsdp"), "tensor"),
        P(("engine", "fsdp"), None),
        P(None, "tensor"),
        P("tensor", ("engine", "fsdp"), None),
        P(None, "tensor", ("engine", "fsdp")),
        P("tensor", None),
        P(None, "tensor", ("engine", "fsdp")),
        P(("engine", "fsdp"), None, None),
        P(("engine", "fsdp"), None, None),
        P(("engine", "fsdp"), None),
        P(("engine", "fsdp")),
    )
    out_specs = P(("engine", "fsdp"), "tensor")
    shape = dict(mesh.shape)
    paired = shape["tensor"] == 2 and shape["engine"] == 4
    body = functools.partial(per_device, shape["fsdp"]) if paired else per_device_plain
    return jax.shard_map(
        body, mesh=mesh, in_specs=in_specs, out_specs=out_specs, check_vma=False
    )
```

```python
import functools

import jax
import jax.numpy as jnp
from jax import lax
from jax.experimental import pallas as pl
from jax.experimental.pallas import tpu as pltpu
from jax.sharding import PartitionSpec as P

MESH = pl.DeviceIdType.MESH
KV, QUERY, OUT = 0, 1, 2
SIB, CROSS, LEFT, RIGHT = 0, 1, 2, 3


def rotate(values, places):
    half = values.shape[-1] // 2
    index = jnp.arange(half).astype(jnp.float32)
    inverse = jnp.exp(index * (-2.0 / values.shape[-1]) * jnp.log(jnp.float32(500000.0)))
    angle = places.astype(jnp.float32)[:, None] * inverse[None, :]
    cosine = jnp.cos(angle)
    sine = jnp.sin(angle)
    first = values[:, :half]
    second = values[:, half:]
    return jnp.concatenate([first * cosine - second * sine, second * cosine + first * sine], axis=1)


def attend(query, new_keys, new_values, old_keys, old_values, offset):
    tok_count = query.shape[0]
    slots = old_keys.shape[0]
    keys_all = jnp.concatenate([old_keys, new_keys], axis=0)
    values_all = jnp.concatenate([old_values, new_values], axis=0)
    scores = jnp.dot(query, keys_all.T, preferred_element_type=jnp.float32) * query.shape[-1] ** (
        -0.5
    )
    slot_seen = jnp.broadcast_to(jnp.arange(slots)[None, :] < offset, (tok_count, slots))
    rows = jnp.arange(tok_count)
    new_seen = rows[None, :] <= rows[:, None]
    seen = jnp.concatenate([slot_seen, new_seen], axis=1)
    scores = jnp.where(seen, scores, jnp.float32(-1e30))
    top = jnp.max(scores, axis=1, keepdims=True)
    probs = jnp.exp(scores - top)
    weights = (probs / jnp.sum(probs, axis=1, keepdims=True)).astype(jnp.bfloat16)
    return jnp.dot(weights, values_all, preferred_element_type=jnp.float32).astype(jnp.bfloat16)


def per_device_plain(
    layer_input,
    norm_gain,
    query_base,
    query_down,
    query_up,
    kv_base,
    output_base_weight,
    output_down_factor,
    output_up_factor,
    cache_keys,
    cache_values,
    positions,
    offsets,
):
    head_size = query_base.shape[1]
    tok_count = layer_input.shape[0]
    full_input, full_gain, complete_down_factor = (
        lax.all_gather(layer_input, "tensor", axis=1, tiled=True),
        lax.all_gather(norm_gain, "tensor", axis=0, tiled=True),
        lax.all_gather(output_down_factor, "tensor", axis=0, tiled=True),
    )
    wide = full_input.astype(jnp.float32)
    scale = lax.rsqrt(jnp.mean(wide * wide, axis=1, keepdims=True) + 1e-05)
    normed = (wide * scale * full_gain.astype(jnp.float32)[None, :]).astype(jnp.bfloat16)
    local_normed = (
        layer_input.astype(jnp.float32) * scale * norm_gain.astype(jnp.float32)[None, :]
    ).astype(jnp.bfloat16)
    merged_query = (
        query_base.astype(jnp.float32)
        + 2.0 * jnp.dot(query_down, query_up, preferred_element_type=jnp.float32)
    ).astype(jnp.bfloat16)
    columns = normed
    query_raw = jnp.dot(
        columns,
        lax.all_gather(merged_query, ("engine", "fsdp"), axis=0, tiled=True),
        preferred_element_type=jnp.float32,
    )
    columns = local_normed
    kv_part = jnp.dot(
        columns,
        lax.all_gather(kv_base, ("engine", "fsdp"), axis=1, tiled=True)[0],
        preferred_element_type=jnp.float32,
    )
    kv_total = lax.psum(kv_part.astype(jnp.bfloat16), "tensor").astype(jnp.float32)
    places = positions[0]
    query = rotate(query_raw, places).astype(jnp.bfloat16)
    new_keys = rotate(kv_total[:, :head_size], places).astype(jnp.bfloat16)
    new_values = kv_total[:, head_size:].astype(jnp.bfloat16)
    head_out = attend(query, new_keys, new_values, cache_keys[0], cache_values[0], offsets[0])
    adapter_output_delta = jnp.einsum(
        "lz,zam->lam",
        complete_down_factor.astype(jnp.float32),
        output_up_factor.astype(jnp.float32),
    )
    combined_output_weight = (
        output_base_weight.astype(jnp.float32) + 2.0 * adapter_output_delta
    ).astype(jnp.bfloat16)
    own_rows = lax.all_to_all(
        combined_output_weight, "tensor", split_axis=0, concat_axis=1, tiled=True
    )
    terms = jnp.einsum(
        "tk,kbn->tbn",
        head_out,
        lax.all_gather(own_rows, ("engine", "fsdp"), axis=2, tiled=True),
        preferred_element_type=jnp.float32,
    )
    flat_terms = terms.reshape(tok_count, terms.shape[1] * terms.shape[2])
    attended = lax.psum_scatter(
        flat_terms.astype(jnp.bfloat16), "tensor", scatter_dimension=1, tiled=True
    )
    return attended


def kernel(
    n_f,
    input_hbm,
    gain_hbm,
    qbase_hbm,
    qdown_hbm,
    qup_hbm,
    kvbase_hbm,
    obase_hbm,
    odown_hbm,
    oup_hbm,
    ckeys_hbm,
    cvalues_hbm,
    places_hbm,
    offset_ref,
    result_ref,
    input_ref,
    gain_ref,
    qbase_ref,
    qdown_ref,
    qup_ref,
    obase_ref,
    odown_ref,
    oup_ref,
    ckeys_ref,
    cvalues_ref,
    places_ref,
    kv_buf,
    q_buf,
    o_buf,
    normed,
    squares,
    down_full,
    kv_part,
    q_total,
    heads,
    cosine_ref,
    sine_ref,
    recv_sem,
    send_sem,
    y_recv,
    y_send,
    n_recv,
    n_send,
    load_sem,
):
    engine = lax.axis_index("engine")
    z = lax.axis_index("fsdp")
    t = lax.axis_index("tensor")
    core = lax.rem(engine, 2)
    sibling = engine + 1 - 2 * core
    across = lax.rem(engine + 2, 4)
    other = 1 - t
    bufs = (kv_buf, q_buf, o_buf)
    groups = 4 * n_f
    tok = input_ref.shape[0]
    head = qbase_ref.shape[1]
    piece = kvbase_hbm.shape[0]
    half_groups = groups // 2
    mine = engine * n_f + z
    width = 2 * input_ref.shape[1]

    def copy(m, g, way):
        target = {
            SIB: (sibling, z, t),
            CROSS: (across, z, t),
            LEFT: (engine, jnp.maximum(z - 1, 0), t),
            RIGHT: (engine, jnp.minimum(z + 1, n_f - 1), t),
        }[way]
        return pltpu.make_async_remote_copy(
            src_ref=bufs[m].at[g],
            dst_ref=bufs[m].at[g],
            send_sem=send_sem.at[m, way, g],
            recv_sem=recv_sem.at[m, g],
            device_id=target,
            device_id_type=MESH,
        )

    def to_partner(ref, k):
        return pltpu.make_async_remote_copy(
            src_ref=ref.at[t],
            dst_ref=ref.at[t],
            send_sem=y_send.at[k],
            recv_sem=y_recv.at[k],
            device_id=(engine, z, other),
            device_id_type=MESH,
        )

    def from_partner(ref, k):
        return pltpu.make_async_remote_copy(
            src_ref=ref.at[other],
            dst_ref=ref.at[other],
            send_sem=y_send.at[k],
            recv_sem=y_recv.at[k],
            device_id=(engine, z, other),
            device_id_type=MESH,
        )

    def normed_copy(side, k):
        rows = normed.at[pl.ds(side * groups + 2 * k, 2)]
        return pltpu.make_async_remote_copy(
            src_ref=rows,
            dst_ref=rows,
            send_sem=n_send.at[k],
            recv_sem=n_recv.at[k],
            device_id=(engine, z, other),
            device_id_type=MESH,
        )

    def own(m):
        g = engine * n_f + z
        copy(m, g, CROSS).start()

        @pl.when(z > 0)
        def _():
            copy(m, g, LEFT).start()

        @pl.when(z < n_f - 1)
        def _():
            copy(m, g, RIGHT).start()

        copy(m, g, SIB).start()

    early = (n_f // 2 - 1, n_f // 2)

    def relay_cross(m, g, zz):
        if m == KV:
            pl.when((zz != early[0]) & (zz != early[1]))(lambda: copy(m, g, CROSS).start())
        else:
            copy(m, g, CROSS).start()

    def along(m, d):
        @pl.when(z >= d)
        def _():
            g = engine * n_f + z - d
            copy(m, g, SIB).wait_recv()

            @pl.when(z < n_f - 1)
            def _():
                copy(m, g, RIGHT).start()

            relay_cross(m, g, z - d)
            copy(m, g, SIB).start()

        @pl.when(z + d < n_f)
        def _():
            g = engine * n_f + z + d
            copy(m, g, SIB).wait_recv()

            @pl.when(z > 0)
            def _():
                copy(m, g, LEFT).start()

            relay_cross(m, g, z + d)
            copy(m, g, SIB).start()

    def crossing(m, d):
        def take(zz):
            g = across * n_f + zz
            copy(m, g, SIB).wait_recv()
            copy(m, g, SIB).start()

        def late(zz):
            return (zz != early[0]) & (zz != early[1]) if m == KV else zz >= 0

        if d == 0:
            take(z)
            if m == KV:
                g = across * n_f + z

                @pl.when(((z == early[0]) | (z == early[1])) & (z > 0))
                def _():
                    copy(m, g, LEFT).start()

                @pl.when(((z == early[0]) | (z == early[1])) & (z < n_f - 1))
                def _():
                    copy(m, g, RIGHT).start()

        else:
            pl.when((z >= d) & late(z - d))(lambda: take(z - d))
            pl.when((z + d < n_f) & late(z + d))(lambda: take(z + d))

    def far(m):
        for k in range(2):
            zz = jnp.where(z < n_f // 2, early[k], early[1 - k])
            g = across * n_f + zz

            @pl.when(z != zz)
            def _(g=g, zz=zz):
                copy(m, g, SIB).wait_recv()
                copy(m, g, SIB).start()

                @pl.when((z < zz) & (z > 0))
                def _():
                    copy(m, g, LEFT).start()

                @pl.when((z > zz) & (z < n_f - 1))
                def _():
                    copy(m, g, RIGHT).start()

    def from_sibling(m):
        def both(k, carry):
            copy(m, sibling * n_f + k, SIB).wait_recv()
            copy(m, lax.rem(sibling + 2, 4) * n_f + k, SIB).wait_recv()
            return carry

        lax.fori_loop(0, n_f, both, 0)

    loads = [
        pltpu.make_async_copy(source, target, load_sem.at[k])
        for k, (source, target) in enumerate(
            (
                (kvbase_hbm, kv_buf.at[mine]),
                (odown_hbm, odown_ref),
                (input_hbm, input_ref),
                (qbase_hbm, qbase_ref),
                (qdown_hbm, qdown_ref),
                (qup_hbm, qup_ref),
                (gain_hbm, gain_ref),
                (obase_hbm, obase_ref),
                (oup_hbm, oup_ref),
                (places_hbm, places_ref),
                (ckeys_hbm, ckeys_ref),
                (cvalues_hbm, cvalues_ref),
            )
        )
    ]
    for load in loads:
        load.start()

    barrier = pltpu.get_barrier_semaphore()

    def greet(target):
        pl.semaphore_signal(barrier, inc=1, device_id=target, device_id_type=MESH)

    greet((sibling, z, t))
    greet((across, z, t))
    greet((engine, z, other))
    pl.when(z > 0)(lambda: greet((engine, z - 1, t)))
    pl.when(z < n_f - 1)(lambda: greet((engine, z + 1, t)))

    loads[0].wait()
    loads[1].wait()
    down_full[t] = odown_ref[...]
    pl.semaphore_wait(barrier, 5 - (z == 0).astype(jnp.int32) - (z == n_f - 1).astype(jnp.int32))

    own(KV)
    to_partner(down_full, 1).start()
    loads[2].wait()
    total = jnp.zeros((tok, 128), jnp.float32)
    for k in range(input_ref.shape[1] // 128):
        wide = input_ref[:, k * 128 : (k + 1) * 128].astype(jnp.float32)
        total = total + wide * wide
    squares[t] = total
    to_partner(squares, 0).start()

    over_rank = (((0,), (0,)), ((), ()))
    for k in range(3, 6):
        loads[k].wait()
    q_buf[mine] = (
        qbase_ref[...].astype(jnp.float32)
        + 2.0
        * lax.dot_general(
            qdown_ref[...], qup_ref[...], over_rank, preferred_element_type=jnp.float32
        )
    ).astype(jnp.bfloat16)
    own(QUERY)

    loads[6].wait()
    from_partner(squares, 0).wait_recv()
    mean = jnp.sum(squares[0] + squares[1], axis=1, keepdims=True) * (1.0 / width)
    scale = jnp.broadcast_to(lax.rsqrt(mean + 1e-05), (tok, 128))
    each = piece // 128
    for k in range(groups):
        for part in range(each):
            at = k * each + part
            normed[t * groups + k, :, part * 128 : (part + 1) * 128] = (
                input_ref[:, at * 128 : (at + 1) * 128].astype(jnp.float32)
                * scale
                * gain_ref[at : at + 1, :].astype(jnp.float32)
            ).astype(jnp.bfloat16)
        if k % 2 == 1:
            normed_copy(t, k // 2).start()

    for k in range(7, len(loads)):
        loads[k].wait()

    crossing(KV, 0)
    along(KV, 1)
    along(KV, 2)

    from_partner(down_full, 1).wait_recv()
    for side in range(2):
        rows = slice(side * head, (side + 1) * head)
        o_buf[mine, rows, :] = (
            obase_ref[rows, :].astype(jnp.float32)
            + 2.0
            * lax.dot_general(
                down_full[side], oup_ref[...], over_rank, preferred_element_type=jnp.float32
            )
        ).astype(jnp.bfloat16)
    own(OUT)

    far(KV)
    along(QUERY, 1)
    along(KV, 3)

    lane = lax.broadcasted_iota(jnp.int32, (tok, head), 1)
    low = lane < head // 2
    index = jnp.where(low, lane, lane - head // 2).astype(jnp.float32)
    inverse = jnp.exp(index * (-2.0 / head) * jnp.log(jnp.full((tok, head), 500000.0, jnp.float32)))
    places = jnp.broadcast_to(places_ref[...].astype(jnp.float32), (head, tok)).T
    angle = places * inverse
    cosine_ref[...] = jnp.cos(angle)
    sine_ref[...] = jnp.where(low, -jnp.sin(angle), jnp.sin(angle))

    def rope(values):
        return values * cosine_ref[...] + pltpu.roll(values, head // 2, 1) * sine_ref[...]

    along(QUERY, 2)
    along(QUERY, 3)
    crossing(KV, 1)
    crossing(KV, 2)
    crossing(KV, 3)
    along(OUT, 1)
    crossing(QUERY, 0)
    from_sibling(KV)
    kv_part[t] = jnp.zeros(kv_part.shape[1:], jnp.float32)

    def kv_step(g, carry):
        kv_part[t] += jnp.dot(
            normed[t * groups + g], kv_buf[g], preferred_element_type=jnp.float32
        )
        return carry

    lax.fori_loop(0, groups // 2, kv_step, 0)
    along(OUT, 2)
    lax.fori_loop(groups // 2, groups, kv_step, 0)
    to_partner(kv_part, 2).start()
    along(OUT, 3)
    crossing(QUERY, 1)
    crossing(QUERY, 2)
    crossing(QUERY, 3)
    crossing(OUT, 0)

    from_sibling(QUERY)
    q_total[...] = jnp.zeros_like(q_total)

    def q_step(g):
        q_total[...] += jnp.dot(
            normed[2 * g], q_buf[g, :piece, :], preferred_element_type=jnp.float32
        ) + jnp.dot(normed[2 * g + 1], q_buf[g, piece:, :], preferred_element_type=jnp.float32)

    def q_near(k, carry):
        q_step(t * half_groups + k)
        return carry

    def q_far(k, carry):
        normed_copy(other, k).wait_recv()
        q_step(other * half_groups + k)
        return carry

    lax.fori_loop(0, half_groups, q_near, 0)
    crossing(OUT, 1)
    lax.fori_loop(0, half_groups, q_far, 0)

    query = rope(q_total[...]).astype(jnp.bfloat16)
    from_partner(kv_part, 2).wait_recv()
    kv = kv_part[0] + kv_part[1]
    new_keys = rope(kv[:, :head]).astype(jnp.bfloat16)
    new_values = kv[:, head:].astype(jnp.bfloat16)
    dims = (((1,), (1,)), ((), ()))
    slots = ckeys_ref.shape[0]
    factor = head ** (-0.5)
    old = lax.dot_general(query, ckeys_ref[...], dims, preferred_element_type=jnp.float32) * factor
    new = lax.dot_general(query, new_keys, dims, preferred_element_type=jnp.float32) * factor
    seen = lax.broadcasted_iota(jnp.int32, (tok, slots), 1) < offset_ref[0]
    rows = lax.broadcasted_iota(jnp.int32, (tok, tok), 0)
    columns = lax.broadcasted_iota(jnp.int32, (tok, tok), 1)
    old = jnp.where(seen, old, jnp.float32(-1e30))
    new = jnp.where(columns <= rows, new, jnp.float32(-1e30))
    top = jnp.maximum(
        jnp.max(old, axis=1, keepdims=True), jnp.max(new, axis=1, keepdims=True)
    )
    old = jnp.exp(old - top)
    new = jnp.exp(new - top)
    summed = jnp.sum(old, axis=1, keepdims=True) + jnp.sum(new, axis=1, keepdims=True)
    old = (old / summed).astype(jnp.bfloat16)
    new = (new / summed).astype(jnp.bfloat16)
    heads[t] = (
        jnp.dot(old, cvalues_ref[...], preferred_element_type=jnp.float32)
        + jnp.dot(new, new_values, preferred_element_type=jnp.float32)
    ).astype(jnp.bfloat16)
    to_partner(heads, 3).start()
    from_partner(heads, 3).wait_recv()

    def project(g):
        first = jnp.dot(heads[0], o_buf[g, :head, :], preferred_element_type=jnp.float32)
        second = jnp.dot(heads[1], o_buf[g, head:, :], preferred_element_type=jnp.float32)
        both = first.astype(jnp.bfloat16).astype(jnp.float32) + second.astype(
            jnp.bfloat16
        ).astype(jnp.float32)
        result_ref[:, pl.ds(pl.multiple_of(g * piece, piece), piece)] = both.astype(jnp.bfloat16)

    def column(which):
        def step(k, carry):
            project(which * n_f + k)
            return carry

        lax.fori_loop(0, n_f, step, 0)

    column(engine)
    crossing(OUT, 2)
    crossing(OUT, 3)
    column(across)

    def sibling_column(which):
        def step(k, carry):
            g = which * n_f + k
            copy(OUT, g, SIB).wait_recv()
            project(g)
            return carry

        lax.fori_loop(0, n_f, step, 0)

    sibling_column(sibling)
    sibling_column(lax.rem(sibling + 2, 4))

    for m in range(3):

        def drain(k, carry, m=m):
            g = engine * n_f + k
            copy(m, g, SIB).wait_send()
            far_g = across * n_f + k
            copy(m, far_g, SIB).wait_send()
            first = (k == early[0]) | (k == early[1])
            if m == KV:
                pl.when(~first | (k == z))(lambda: copy(m, g, CROSS).wait_send())

                @pl.when(first & (z > 0) & (k >= z))
                def _():
                    copy(m, far_g, LEFT).wait_send()

                @pl.when(first & (z < n_f - 1) & (k <= z))
                def _():
                    copy(m, far_g, RIGHT).wait_send()

            else:
                copy(m, g, CROSS).wait_send()

            @pl.when((z > 0) & (k >= z))
            def _():
                copy(m, g, LEFT).wait_send()

            @pl.when((z < n_f - 1) & (k <= z))
            def _():
                copy(m, g, RIGHT).wait_send()

            return carry

        lax.fori_loop(0, n_f, drain, 0)

    def drain_normed(k, carry):
        normed_copy(t, k).wait_send()
        return carry

    lax.fori_loop(0, half_groups, drain_normed, 0)
    to_partner(squares, 0).wait_send()
    to_partner(down_full, 1).wait_send()
    to_partner(kv_part, 2).wait_send()
    to_partner(heads, 3).wait_send()


def per_device(
    n_f,
    layer_input,
    norm_gain,
    query_base,
    query_down,
    query_up,
    kv_base,
    output_base_weight,
    output_down_factor,
    output_up_factor,
    cache_keys,
    cache_values,
    positions,
    offsets,
):
    tok, features = layer_input.shape
    depth, head = query_base.shape
    rank = query_up.shape[0]
    groups = 4 * n_f
    kv_base = kv_base[0]
    output_base_weight = output_base_weight[:, 0]
    output_up_factor = output_up_factor[:, 0]
    piece = kv_base.shape[0]
    vmem = pl.BlockSpec(memory_space=pltpu.VMEM)
    hbm = pl.BlockSpec(memory_space=pltpu.HBM)
    smem = pl.BlockSpec(memory_space=pltpu.SMEM)
    dma = pltpu.SemaphoreType.DMA
    return pl.pallas_call(
        functools.partial(kernel, n_f),
        out_shape=jax.ShapeDtypeStruct((tok, features), jnp.bfloat16),
        in_specs=[hbm] * 12 + [smem],
        out_specs=vmem,
        scratch_shapes=[
            pltpu.VMEM((tok, features), jnp.bfloat16),
            pltpu.VMEM((features // 128, 128), jnp.bfloat16),
            pltpu.VMEM(query_base.shape, jnp.bfloat16),
            pltpu.VMEM((rank, depth), jnp.bfloat16),
            pltpu.VMEM(query_up.shape, jnp.bfloat16),
            pltpu.VMEM(output_base_weight.shape, jnp.bfloat16),
            pltpu.VMEM((rank, head), jnp.bfloat16),
            pltpu.VMEM(output_up_factor.shape, jnp.bfloat16),
            pltpu.VMEM(cache_keys.shape[1:], jnp.bfloat16),
            pltpu.VMEM(cache_values.shape[1:], jnp.bfloat16),
            pltpu.VMEM(positions.shape, jnp.int32),
            pltpu.VMEM((groups,) + kv_base.shape, jnp.bfloat16),
            pltpu.VMEM((groups,) + query_base.shape, jnp.bfloat16),
            pltpu.VMEM((groups,) + output_base_weight.shape, jnp.bfloat16),
            pltpu.VMEM((2 * groups, tok, piece), jnp.bfloat16),
            pltpu.VMEM((2, tok, 128), jnp.float32),
            pltpu.VMEM((2, rank, head), jnp.bfloat16),
            pltpu.VMEM((2, tok, 2 * head), jnp.float32),
            pltpu.VMEM((tok, head), jnp.float32),
            pltpu.VMEM((2, tok, head), jnp.bfloat16),
            pltpu.VMEM((tok, head), jnp.float32),
            pltpu.VMEM((tok, head), jnp.float32),
            dma((3, groups)),
            dma((3, 4, groups)),
            dma((4,)),
            dma((4,)),
            dma((groups // 2,)),
            dma((groups // 2,)),
            dma((12,)),
        ],
        compiler_params=pltpu.CompilerParams(
            collective_id=0, has_side_effects=True, vmem_limit_bytes=60 * 1024 * 1024
        ),
    )(
        layer_input,
        norm_gain.reshape(-1, 128),
        query_base,
        query_down.T,
        query_up,
        kv_base,
        output_base_weight,
        output_down_factor.T,
        output_up_factor,
        cache_keys[0],
        cache_values[0],
        positions,
        offsets,
    )


def solution(mesh):
    in_specs = (
        P(("engine", "fsdp"), "tensor"),
        P("tensor"),
        P(("engine", "fsdp"), "tensor"),
        P(("engine", "fsdp"), None),
        P(None, "tensor"),
        P("tensor", ("engine", "fsdp"), None),
        P(None, "tensor", ("engine", "fsdp")),
        P("tensor", None),
        P(None, "tensor", ("engine", "fsdp")),
        P(("engine", "fsdp"), None, None),
        P(("engine", "fsdp"), None, None),
        P(("engine", "fsdp"), None),
        P(("engine", "fsdp")),
    )
    out_specs = P(("engine", "fsdp"), "tensor")
    shape = dict(mesh.shape)
    paired = shape["tensor"] == 2 and shape["engine"] == 4
    body = functools.partial(per_device, shape["fsdp"]) if paired else per_device_plain
    return jax.shard_map(
        body, mesh=mesh, in_specs=in_specs, out_specs=out_specs, check_vma=False
    )
```

```python
import functools

import jax
import jax.numpy as jnp
from jax import lax
from jax.experimental import pallas as pl
from jax.experimental.pallas import tpu as pltpu
from jax.sharding import PartitionSpec as P

MESH = pl.DeviceIdType.MESH
KV, QUERY, OUT = 0, 1, 2
SIB, CROSS, LEFT, RIGHT = 0, 1, 2, 3


def rotate(values, places):
    half = values.shape[-1] // 2
    index = jnp.arange(half).astype(jnp.float32)
    inverse = jnp.exp(index * (-2.0 / values.shape[-1]) * jnp.log(jnp.float32(500000.0)))
    angle = places.astype(jnp.float32)[:, None] * inverse[None, :]
    cosine = jnp.cos(angle)
    sine = jnp.sin(angle)
    first = values[:, :half]
    second = values[:, half:]
    return jnp.concatenate([first * cosine - second * sine, second * cosine + first * sine], axis=1)


def attend(query, new_keys, new_values, old_keys, old_values, offset):
    tok_count = query.shape[0]
    slots = old_keys.shape[0]
    keys_all = jnp.concatenate([old_keys, new_keys], axis=0)
    values_all = jnp.concatenate([old_values, new_values], axis=0)
    scores = jnp.dot(query, keys_all.T, preferred_element_type=jnp.float32) * query.shape[-1] ** (
        -0.5
    )
    slot_seen = jnp.broadcast_to(jnp.arange(slots)[None, :] < offset, (tok_count, slots))
    rows = jnp.arange(tok_count)
    new_seen = rows[None, :] <= rows[:, None]
    seen = jnp.concatenate([slot_seen, new_seen], axis=1)
    scores = jnp.where(seen, scores, jnp.float32(-1e30))
    top = jnp.max(scores, axis=1, keepdims=True)
    probs = jnp.exp(scores - top)
    weights = (probs / jnp.sum(probs, axis=1, keepdims=True)).astype(jnp.bfloat16)
    return jnp.dot(weights, values_all, preferred_element_type=jnp.float32).astype(jnp.bfloat16)


def per_device_plain(
    layer_input,
    norm_gain,
    query_base,
    query_down,
    query_up,
    kv_base,
    output_base_weight,
    output_down_factor,
    output_up_factor,
    cache_keys,
    cache_values,
    positions,
    offsets,
):
    head_size = query_base.shape[1]
    tok_count = layer_input.shape[0]
    full_input, full_gain, complete_down_factor = (
        lax.all_gather(layer_input, "tensor", axis=1, tiled=True),
        lax.all_gather(norm_gain, "tensor", axis=0, tiled=True),
        lax.all_gather(output_down_factor, "tensor", axis=0, tiled=True),
    )
    wide = full_input.astype(jnp.float32)
    scale = lax.rsqrt(jnp.mean(wide * wide, axis=1, keepdims=True) + 1e-05)
    normed = (wide * scale * full_gain.astype(jnp.float32)[None, :]).astype(jnp.bfloat16)
    local_normed = (
        layer_input.astype(jnp.float32) * scale * norm_gain.astype(jnp.float32)[None, :]
    ).astype(jnp.bfloat16)
    merged_query = (
        query_base.astype(jnp.float32)
        + 2.0 * jnp.dot(query_down, query_up, preferred_element_type=jnp.float32)
    ).astype(jnp.bfloat16)
    columns = normed
    query_raw = jnp.dot(
        columns,
        lax.all_gather(merged_query, ("engine", "fsdp"), axis=0, tiled=True),
        preferred_element_type=jnp.float32,
    )
    columns = local_normed
    kv_part = jnp.dot(
        columns,
        lax.all_gather(kv_base, ("engine", "fsdp"), axis=1, tiled=True)[0],
        preferred_element_type=jnp.float32,
    )
    kv_total = lax.psum(kv_part.astype(jnp.bfloat16), "tensor").astype(jnp.float32)
    places = positions[0]
    query = rotate(query_raw, places).astype(jnp.bfloat16)
    new_keys = rotate(kv_total[:, :head_size], places).astype(jnp.bfloat16)
    new_values = kv_total[:, head_size:].astype(jnp.bfloat16)
    head_out = attend(query, new_keys, new_values, cache_keys[0], cache_values[0], offsets[0])
    adapter_output_delta = jnp.einsum(
        "lz,zam->lam",
        complete_down_factor.astype(jnp.float32),
        output_up_factor.astype(jnp.float32),
    )
    combined_output_weight = (
        output_base_weight.astype(jnp.float32) + 2.0 * adapter_output_delta
    ).astype(jnp.bfloat16)
    own_rows = lax.all_to_all(
        combined_output_weight, "tensor", split_axis=0, concat_axis=1, tiled=True
    )
    terms = jnp.einsum(
        "tk,kbn->tbn",
        head_out,
        lax.all_gather(own_rows, ("engine", "fsdp"), axis=2, tiled=True),
        preferred_element_type=jnp.float32,
    )
    flat_terms = terms.reshape(tok_count, terms.shape[1] * terms.shape[2])
    attended = lax.psum_scatter(
        flat_terms.astype(jnp.bfloat16), "tensor", scatter_dimension=1, tiled=True
    )
    return attended


def kernel(
    n_f,
    input_hbm,
    gain_hbm,
    qbase_hbm,
    qdown_hbm,
    qup_hbm,
    kvbase_hbm,
    obase_hbm,
    odown_hbm,
    oup_hbm,
    ckeys_hbm,
    cvalues_hbm,
    places_hbm,
    offset_ref,
    result_ref,
    input_ref,
    gain_ref,
    qbase_ref,
    qdown_ref,
    qup_ref,
    obase_ref,
    odown_ref,
    oup_ref,
    ckeys_ref,
    cvalues_ref,
    places_ref,
    kv_buf,
    q_buf,
    o_buf,
    normed,
    squares,
    down_full,
    kv_part,
    q_total,
    heads,
    both,
    cosine_ref,
    sine_ref,
    recv_sem,
    send_sem,
    y_recv,
    y_send,
    n_recv,
    n_send,
    load_sem,
):
    engine = lax.axis_index("engine")
    z = lax.axis_index("fsdp")
    t = lax.axis_index("tensor")
    core = lax.rem(engine, 2)
    sibling = engine + 1 - 2 * core
    across = lax.rem(engine + 2, 4)
    other = 1 - t
    bufs = (kv_buf, q_buf, o_buf)
    groups = 4 * n_f
    tok = input_ref.shape[0]
    head = qbase_ref.shape[1]
    piece = kvbase_hbm.shape[0]
    half_groups = groups // 2
    mine = engine * n_f + z
    width = 2 * input_ref.shape[1]

    def copy(m, g, way):
        target = {
            SIB: (sibling, z, t),
            CROSS: (across, z, t),
            LEFT: (engine, jnp.maximum(z - 1, 0), t),
            RIGHT: (engine, jnp.minimum(z + 1, n_f - 1), t),
        }[way]
        return pltpu.make_async_remote_copy(
            src_ref=bufs[m].at[g],
            dst_ref=bufs[m].at[g],
            send_sem=send_sem.at[m, way, g],
            recv_sem=recv_sem.at[m, g],
            device_id=target,
            device_id_type=MESH,
        )

    def to_partner(ref, k):
        return pltpu.make_async_remote_copy(
            src_ref=ref.at[t],
            dst_ref=ref.at[t],
            send_sem=y_send.at[k],
            recv_sem=y_recv.at[k],
            device_id=(engine, z, other),
            device_id_type=MESH,
        )

    def from_partner(ref, k):
        return pltpu.make_async_remote_copy(
            src_ref=ref.at[other],
            dst_ref=ref.at[other],
            send_sem=y_send.at[k],
            recv_sem=y_recv.at[k],
            device_id=(engine, z, other),
            device_id_type=MESH,
        )

    def normed_copy(side, k):
        rows = normed.at[pl.ds(side * groups + 2 * k, 2)]
        return pltpu.make_async_remote_copy(
            src_ref=rows,
            dst_ref=rows,
            send_sem=n_send.at[k],
            recv_sem=n_recv.at[k],
            device_id=(engine, z, other),
            device_id_type=MESH,
        )

    def own(m):
        g = engine * n_f + z
        copy(m, g, CROSS).start()

        @pl.when(z > 0)
        def _():
            copy(m, g, LEFT).start()

        @pl.when(z < n_f - 1)
        def _():
            copy(m, g, RIGHT).start()

        copy(m, g, SIB).start()

    def along(m, d):
        @pl.when(z >= d)
        def _():
            g = engine * n_f + z - d
            copy(m, g, SIB).wait_recv()

            @pl.when(z < n_f - 1)
            def _():
                copy(m, g, RIGHT).start()

            copy(m, g, CROSS).start()
            copy(m, g, SIB).start()

        @pl.when(z + d < n_f)
        def _():
            g = engine * n_f + z + d
            copy(m, g, SIB).wait_recv()

            @pl.when(z > 0)
            def _():
                copy(m, g, LEFT).start()

            copy(m, g, CROSS).start()
            copy(m, g, SIB).start()

    def crossing(m, d):
        def take(zz):
            g = across * n_f + zz
            copy(m, g, SIB).wait_recv()
            copy(m, g, SIB).start()

        if d == 0:
            take(z)
        else:
            pl.when(z >= d)(lambda: take(z - d))
            pl.when(z + d < n_f)(lambda: take(z + d))

    def from_sibling(m):
        def arrived(k, carry):
            copy(m, sibling * n_f + k, SIB).wait_recv()
            copy(m, lax.rem(sibling + 2, 4) * n_f + k, SIB).wait_recv()
            return carry

        lax.fori_loop(0, n_f, arrived, 0)

    loads = [
        pltpu.make_async_copy(source, target, load_sem.at[k])
        for k, (source, target) in enumerate(
            (
                (kvbase_hbm, kv_buf.at[mine]),
                (odown_hbm, odown_ref),
                (input_hbm, input_ref),
                (qbase_hbm, qbase_ref),
                (qdown_hbm, qdown_ref),
                (qup_hbm, qup_ref),
                (gain_hbm, gain_ref),
                (obase_hbm, obase_ref),
                (oup_hbm, oup_ref),
                (places_hbm, places_ref),
                (ckeys_hbm, ckeys_ref),
                (cvalues_hbm, cvalues_ref),
            )
        )
    ]
    for load in loads:
        load.start()

    barrier = pltpu.get_barrier_semaphore()

    def greet(target):
        pl.semaphore_signal(barrier, inc=1, device_id=target, device_id_type=MESH)

    greet((sibling, z, t))
    greet((across, z, t))
    greet((engine, z, other))
    pl.when(z > 0)(lambda: greet((engine, z - 1, t)))
    pl.when(z < n_f - 1)(lambda: greet((engine, z + 1, t)))

    loads[0].wait()
    loads[1].wait()
    down_full[t] = odown_ref[...]
    pl.semaphore_wait(barrier, 5 - (z == 0).astype(jnp.int32) - (z == n_f - 1).astype(jnp.int32))

    own(KV)
    to_partner(down_full, 1).start()
    loads[2].wait()
    total = jnp.zeros((tok, 128), jnp.float32)
    for k in range(input_ref.shape[1] // 128):
        wide = input_ref[:, k * 128 : (k + 1) * 128].astype(jnp.float32)
        total = total + wide * wide
    squares[t] = total
    to_partner(squares, 0).start()

    over_rank = (((0,), (0,)), ((), ()))
    for k in range(3, 6):
        loads[k].wait()
    q_buf[mine] = (
        qbase_ref[...].astype(jnp.float32)
        + 2.0
        * lax.dot_general(
            qdown_ref[...], qup_ref[...], over_rank, preferred_element_type=jnp.float32
        )
    ).astype(jnp.bfloat16)
    own(QUERY)

    loads[6].wait()
    from_partner(squares, 0).wait_recv()
    mean = jnp.sum(squares[0] + squares[1], axis=1, keepdims=True) * (1.0 / width)
    scale = jnp.broadcast_to(lax.rsqrt(mean + 1e-05), (tok, 128))
    each = piece // 128
    for k in range(groups):
        for part in range(each):
            at = k * each + part
            normed[t * groups + k, :, part * 128 : (part + 1) * 128] = (
                input_ref[:, at * 128 : (at + 1) * 128].astype(jnp.float32)
                * scale
                * gain_ref[at : at + 1, :].astype(jnp.float32)
            ).astype(jnp.bfloat16)
        if k % 2 == 1:
            normed_copy(t, k // 2).start()

    for k in range(7, len(loads)):
        loads[k].wait()

    along(KV, 1)
    along(KV, 2)

    from_partner(down_full, 1).wait_recv()
    for side in range(2):
        rows = slice(side * head, (side + 1) * head)
        o_buf[mine, rows, :] = (
            obase_ref[rows, :].astype(jnp.float32)
            + 2.0
            * lax.dot_general(
                down_full[side], oup_ref[...], over_rank, preferred_element_type=jnp.float32
            )
        ).astype(jnp.bfloat16)
    own(OUT)

    along(QUERY, 1)
    along(KV, 3)
    crossing(KV, 0)

    lane = lax.broadcasted_iota(jnp.int32, (tok, head), 1)
    low = lane < head // 2
    index = jnp.where(low, lane, lane - head // 2).astype(jnp.float32)
    inverse = jnp.exp(index * (-2.0 / head) * jnp.log(jnp.full((tok, head), 500000.0, jnp.float32)))
    places = jnp.broadcast_to(places_ref[...].astype(jnp.float32), (head, tok)).T
    angle = places * inverse
    cosine_ref[...] = jnp.cos(angle)
    sine_ref[...] = jnp.where(low, -jnp.sin(angle), jnp.sin(angle))

    def rope(values):
        return values * cosine_ref[...] + pltpu.roll(values, head // 2, 1) * sine_ref[...]

    along(QUERY, 2)
    crossing(KV, 1)
    along(QUERY, 3)
    crossing(KV, 2)
    along(OUT, 1)
    crossing(KV, 3)
    crossing(QUERY, 0)
    along(OUT, 2)
    from_sibling(KV)
    kv_part[t] = jnp.zeros(kv_part.shape[1:], jnp.float32)

    def kv_step(g, carry):
        kv_part[t] += jnp.dot(
            normed[t * groups + g], kv_buf[g], preferred_element_type=jnp.float32
        )
        return carry

    lax.fori_loop(0, groups // 2, kv_step, 0)
    crossing(QUERY, 1)
    along(OUT, 3)
    lax.fori_loop(groups // 2, groups, kv_step, 0)
    to_partner(kv_part, 2).start()
    crossing(QUERY, 2)
    crossing(QUERY, 3)
    crossing(OUT, 0)

    from_sibling(QUERY)
    q_total[...] = jnp.zeros_like(q_total)

    def q_step(g):
        q_total[...] += jnp.dot(
            normed[2 * g], q_buf[g, :piece, :], preferred_element_type=jnp.float32
        ) + jnp.dot(normed[2 * g + 1], q_buf[g, piece:, :], preferred_element_type=jnp.float32)

    def q_near(k, carry):
        q_step(t * half_groups + k)
        return carry

    def q_far(k, carry):
        normed_copy(other, k).wait_recv()
        q_step(other * half_groups + k)
        return carry

    lax.fori_loop(0, half_groups, q_near, 0)
    crossing(OUT, 1)
    lax.fori_loop(0, half_groups, q_far, 0)

    query = rope(q_total[...]).astype(jnp.bfloat16)
    from_partner(kv_part, 2).wait_recv()
    kv = kv_part[0] + kv_part[1]
    new_keys = rope(kv[:, :head]).astype(jnp.bfloat16)
    new_values = kv[:, head:].astype(jnp.bfloat16)
    dims = (((1,), (1,)), ((), ()))
    slots = ckeys_ref.shape[0]
    factor = head ** (-0.5)
    old = lax.dot_general(query, ckeys_ref[...], dims, preferred_element_type=jnp.float32) * factor
    new = lax.dot_general(query, new_keys, dims, preferred_element_type=jnp.float32) * factor
    seen = lax.broadcasted_iota(jnp.int32, (tok, slots), 1) < offset_ref[0]
    rows = lax.broadcasted_iota(jnp.int32, (tok, tok), 0)
    columns = lax.broadcasted_iota(jnp.int32, (tok, tok), 1)
    old = jnp.where(seen, old, jnp.float32(-1e30))
    new = jnp.where(columns <= rows, new, jnp.float32(-1e30))
    top = jnp.maximum(
        jnp.max(old, axis=1, keepdims=True), jnp.max(new, axis=1, keepdims=True)
    )
    old = jnp.exp(old - top)
    new = jnp.exp(new - top)
    summed = jnp.sum(old, axis=1, keepdims=True) + jnp.sum(new, axis=1, keepdims=True)
    old = (old / summed).astype(jnp.bfloat16)
    new = (new / summed).astype(jnp.bfloat16)
    own_head = (
        jnp.dot(old, cvalues_ref[...], preferred_element_type=jnp.float32)
        + jnp.dot(new, new_values, preferred_element_type=jnp.float32)
    ).astype(jnp.bfloat16)
    heads[t] = own_head
    to_partner(heads, 3).start()
    from_partner(heads, 3).wait_recv()

    both[:, :head] = heads[0]
    both[:, head:] = heads[1]

    def project(g):
        result_ref[:, pl.ds(pl.multiple_of(g * piece, piece), piece)] = jnp.dot(
            both[...], o_buf[g], preferred_element_type=jnp.float32
        ).astype(jnp.bfloat16)

    def near(k, carry):
        project(engine * n_f + k)
        g = sibling * n_f + k
        copy(OUT, g, SIB).wait_recv()
        project(g)
        return carry

    def crossed(d):
        def pair(zz):
            project(across * n_f + zz)
            g = lax.rem(sibling + 2, 4) * n_f + zz
            copy(OUT, g, SIB).wait_recv()
            project(g)

        if d == 0:
            pair(z)
        else:
            pl.when(z >= d)(lambda: pair(z - d))
            pl.when(z + d < n_f)(lambda: pair(z + d))

    lax.fori_loop(0, n_f, near, 0)
    crossing(OUT, 2)
    crossed(0)
    crossed(1)
    crossing(OUT, 3)
    crossed(2)
    crossed(3)

    for m in range(3):

        def drain(k, carry, m=m):
            g = engine * n_f + k
            copy(m, g, SIB).wait_send()
            copy(m, g, CROSS).wait_send()
            copy(m, across * n_f + k, SIB).wait_send()

            @pl.when((z > 0) & (k >= z))
            def _():
                copy(m, g, LEFT).wait_send()

            @pl.when((z < n_f - 1) & (k <= z))
            def _():
                copy(m, g, RIGHT).wait_send()

            return carry

        lax.fori_loop(0, n_f, drain, 0)

    def drain_normed(k, carry):
        normed_copy(t, k).wait_send()
        return carry

    lax.fori_loop(0, half_groups, drain_normed, 0)
    to_partner(squares, 0).wait_send()
    to_partner(down_full, 1).wait_send()
    to_partner(kv_part, 2).wait_send()
    to_partner(heads, 3).wait_send()


def per_device(
    n_f,
    layer_input,
    norm_gain,
    query_base,
    query_down,
    query_up,
    kv_base,
    output_base_weight,
    output_down_factor,
    output_up_factor,
    cache_keys,
    cache_values,
    positions,
    offsets,
):
    tok, features = layer_input.shape
    depth, head = query_base.shape
    rank = query_up.shape[0]
    groups = 4 * n_f
    kv_base = kv_base[0]
    output_base_weight = output_base_weight[:, 0]
    output_up_factor = output_up_factor[:, 0]
    piece = kv_base.shape[0]
    vmem = pl.BlockSpec(memory_space=pltpu.VMEM)
    hbm = pl.BlockSpec(memory_space=pltpu.HBM)
    smem = pl.BlockSpec(memory_space=pltpu.SMEM)
    dma = pltpu.SemaphoreType.DMA
    return pl.pallas_call(
        functools.partial(kernel, n_f),
        out_shape=jax.ShapeDtypeStruct((tok, features), jnp.bfloat16),
        in_specs=[hbm] * 12 + [smem],
        out_specs=vmem,
        scratch_shapes=[
            pltpu.VMEM((tok, features), jnp.bfloat16),
            pltpu.VMEM((features // 128, 128), jnp.bfloat16),
            pltpu.VMEM(query_base.shape, jnp.bfloat16),
            pltpu.VMEM((rank, depth), jnp.bfloat16),
            pltpu.VMEM(query_up.shape, jnp.bfloat16),
            pltpu.VMEM(output_base_weight.shape, jnp.bfloat16),
            pltpu.VMEM((rank, head), jnp.bfloat16),
            pltpu.VMEM(output_up_factor.shape, jnp.bfloat16),
            pltpu.VMEM(cache_keys.shape[1:], jnp.bfloat16),
            pltpu.VMEM(cache_values.shape[1:], jnp.bfloat16),
            pltpu.VMEM(positions.shape, jnp.int32),
            pltpu.VMEM((groups,) + kv_base.shape, jnp.bfloat16),
            pltpu.VMEM((groups,) + query_base.shape, jnp.bfloat16),
            pltpu.VMEM((groups,) + output_base_weight.shape, jnp.bfloat16),
            pltpu.VMEM((2 * groups, tok, piece), jnp.bfloat16),
            pltpu.VMEM((2, tok, 128), jnp.float32),
            pltpu.VMEM((2, rank, head), jnp.bfloat16),
            pltpu.VMEM((2, tok, 2 * head), jnp.float32),
            pltpu.VMEM((tok, head), jnp.float32),
            pltpu.VMEM((2, tok, head), jnp.bfloat16),
            pltpu.VMEM((tok, 2 * head), jnp.bfloat16),
            pltpu.VMEM((tok, head), jnp.float32),
            pltpu.VMEM((tok, head), jnp.float32),
            dma((3, groups)),
            dma((3, 4, groups)),
            dma((4,)),
            dma((4,)),
            dma((groups // 2,)),
            dma((groups // 2,)),
            dma((12,)),
        ],
        compiler_params=pltpu.CompilerParams(
            collective_id=0, has_side_effects=True, vmem_limit_bytes=60 * 1024 * 1024
        ),
    )(
        layer_input,
        norm_gain.reshape(-1, 128),
        query_base,
        query_down.T,
        query_up,
        kv_base,
        output_base_weight,
        output_down_factor.T,
        output_up_factor,
        cache_keys[0],
        cache_values[0],
        positions,
        offsets,
    )


def solution(mesh):
    in_specs = (
        P(("engine", "fsdp"), "tensor"),
        P("tensor"),
        P(("engine", "fsdp"), "tensor"),
        P(("engine", "fsdp"), None),
        P(None, "tensor"),
        P("tensor", ("engine", "fsdp"), None),
        P(None, "tensor", ("engine", "fsdp")),
        P("tensor", None),
        P(None, "tensor", ("engine", "fsdp")),
        P(("engine", "fsdp"), None, None),
        P(("engine", "fsdp"), None, None),
        P(("engine", "fsdp"), None),
        P(("engine", "fsdp")),
    )
    out_specs = P(("engine", "fsdp"), "tensor")
    shape = dict(mesh.shape)
    paired = shape["tensor"] == 2 and shape["engine"] == 4
    body = functools.partial(per_device, shape["fsdp"]) if paired else per_device_plain
    return jax.shard_map(
        body, mesh=mesh, in_specs=in_specs, out_specs=out_specs, check_vma=False
    )
```

```python
import functools

import jax
import jax.numpy as jnp
from jax import lax
from jax.experimental import pallas as pl
from jax.experimental.pallas import tpu as pltpu
from jax.sharding import PartitionSpec as P

MESH = pl.DeviceIdType.MESH
KV, QUERY, OUT = 0, 1, 2
SIB, CROSS, LEFT, RIGHT = 0, 1, 2, 3


def rotate(values, places):
    half = values.shape[-1] // 2
    index = jnp.arange(half).astype(jnp.float32)
    inverse = jnp.exp(index * (-2.0 / values.shape[-1]) * jnp.log(jnp.float32(500000.0)))
    angle = places.astype(jnp.float32)[:, None] * inverse[None, :]
    cosine = jnp.cos(angle)
    sine = jnp.sin(angle)
    first = values[:, :half]
    second = values[:, half:]
    return jnp.concatenate([first * cosine - second * sine, second * cosine + first * sine], axis=1)


def attend(query, new_keys, new_values, old_keys, old_values, offset):
    tok_count = query.shape[0]
    slots = old_keys.shape[0]
    keys_all = jnp.concatenate([old_keys, new_keys], axis=0)
    values_all = jnp.concatenate([old_values, new_values], axis=0)
    scores = jnp.dot(query, keys_all.T, preferred_element_type=jnp.float32) * query.shape[-1] ** (
        -0.5
    )
    slot_seen = jnp.broadcast_to(jnp.arange(slots)[None, :] < offset, (tok_count, slots))
    rows = jnp.arange(tok_count)
    new_seen = rows[None, :] <= rows[:, None]
    seen = jnp.concatenate([slot_seen, new_seen], axis=1)
    scores = jnp.where(seen, scores, jnp.float32(-1e30))
    top = jnp.max(scores, axis=1, keepdims=True)
    probs = jnp.exp(scores - top)
    weights = (probs / jnp.sum(probs, axis=1, keepdims=True)).astype(jnp.bfloat16)
    return jnp.dot(weights, values_all, preferred_element_type=jnp.float32).astype(jnp.bfloat16)


def per_device_plain(
    layer_input,
    norm_gain,
    query_base,
    query_down,
    query_up,
    kv_base,
    output_base_weight,
    output_down_factor,
    output_up_factor,
    cache_keys,
    cache_values,
    positions,
    offsets,
):
    head_size = query_base.shape[1]
    tok_count = layer_input.shape[0]
    full_input, full_gain, complete_down_factor = (
        lax.all_gather(layer_input, "tensor", axis=1, tiled=True),
        lax.all_gather(norm_gain, "tensor", axis=0, tiled=True),
        lax.all_gather(output_down_factor, "tensor", axis=0, tiled=True),
    )
    wide = full_input.astype(jnp.float32)
    scale = lax.rsqrt(jnp.mean(wide * wide, axis=1, keepdims=True) + 1e-05)
    normed = (wide * scale * full_gain.astype(jnp.float32)[None, :]).astype(jnp.bfloat16)
    local_normed = (
        layer_input.astype(jnp.float32) * scale * norm_gain.astype(jnp.float32)[None, :]
    ).astype(jnp.bfloat16)
    merged_query = (
        query_base.astype(jnp.float32)
        + 2.0 * jnp.dot(query_down, query_up, preferred_element_type=jnp.float32)
    ).astype(jnp.bfloat16)
    columns = normed
    query_raw = jnp.dot(
        columns,
        lax.all_gather(merged_query, ("engine", "fsdp"), axis=0, tiled=True),
        preferred_element_type=jnp.float32,
    )
    columns = local_normed
    kv_part = jnp.dot(
        columns,
        lax.all_gather(kv_base, ("engine", "fsdp"), axis=1, tiled=True)[0],
        preferred_element_type=jnp.float32,
    )
    kv_total = lax.psum(kv_part.astype(jnp.bfloat16), "tensor").astype(jnp.float32)
    places = positions[0]
    query = rotate(query_raw, places).astype(jnp.bfloat16)
    new_keys = rotate(kv_total[:, :head_size], places).astype(jnp.bfloat16)
    new_values = kv_total[:, head_size:].astype(jnp.bfloat16)
    head_out = attend(query, new_keys, new_values, cache_keys[0], cache_values[0], offsets[0])
    adapter_output_delta = jnp.einsum(
        "lz,zam->lam",
        complete_down_factor.astype(jnp.float32),
        output_up_factor.astype(jnp.float32),
    )
    combined_output_weight = (
        output_base_weight.astype(jnp.float32) + 2.0 * adapter_output_delta
    ).astype(jnp.bfloat16)
    own_rows = lax.all_to_all(
        combined_output_weight, "tensor", split_axis=0, concat_axis=1, tiled=True
    )
    terms = jnp.einsum(
        "tk,kbn->tbn",
        head_out,
        lax.all_gather(own_rows, ("engine", "fsdp"), axis=2, tiled=True),
        preferred_element_type=jnp.float32,
    )
    flat_terms = terms.reshape(tok_count, terms.shape[1] * terms.shape[2])
    attended = lax.psum_scatter(
        flat_terms.astype(jnp.bfloat16), "tensor", scatter_dimension=1, tiled=True
    )
    return attended


def kernel(
    n_f,
    input_hbm,
    gain_hbm,
    qbase_hbm,
    qdown_hbm,
    qup_hbm,
    kvbase_hbm,
    obase_hbm,
    odown_hbm,
    oup_hbm,
    ckeys_hbm,
    cvalues_hbm,
    places_hbm,
    offset_ref,
    result_ref,
    input_ref,
    gain_ref,
    qbase_ref,
    qdown_ref,
    qup_ref,
    obase_ref,
    odown_ref,
    oup_ref,
    ckeys_ref,
    cvalues_ref,
    places_ref,
    kv_buf,
    q_buf,
    o_buf,
    normed,
    squares,
    down_full,
    kv_part,
    q_total,
    heads,
    both,
    cosine_ref,
    sine_ref,
    recv_sem,
    send_sem,
    y_recv,
    y_send,
    n_recv,
    n_send,
    load_sem,
):
    engine = lax.axis_index("engine")
    z = lax.axis_index("fsdp")
    t = lax.axis_index("tensor")
    core = lax.rem(engine, 2)
    sibling = engine + 1 - 2 * core
    across = lax.rem(engine + 2, 4)
    other = 1 - t
    bufs = (kv_buf, q_buf, o_buf)
    groups = 4 * n_f
    tok = input_ref.shape[0]
    head = qbase_ref.shape[1]
    piece = kvbase_hbm.shape[0]
    half_groups = groups // 2
    mine = engine * n_f + z
    width = 2 * input_ref.shape[1]

    def copy(m, g, way):
        target = {
            SIB: (sibling, z, t),
            CROSS: (across, z, t),
            LEFT: (engine, jnp.maximum(z - 1, 0), t),
            RIGHT: (engine, jnp.minimum(z + 1, n_f - 1), t),
        }[way]
        return pltpu.make_async_remote_copy(
            src_ref=bufs[m].at[g],
            dst_ref=bufs[m].at[g],
            send_sem=send_sem.at[m, way, g],
            recv_sem=recv_sem.at[m, g],
            device_id=target,
            device_id_type=MESH,
        )

    def to_partner(ref, k):
        return pltpu.make_async_remote_copy(
            src_ref=ref.at[t],
            dst_ref=ref.at[t],
            send_sem=y_send.at[k],
            recv_sem=y_recv.at[k],
            device_id=(engine, z, other),
            device_id_type=MESH,
        )

    def from_partner(ref, k):
        return pltpu.make_async_remote_copy(
            src_ref=ref.at[other],
            dst_ref=ref.at[other],
            send_sem=y_send.at[k],
            recv_sem=y_recv.at[k],
            device_id=(engine, z, other),
            device_id_type=MESH,
        )

    def normed_copy(side, k):
        rows = normed.at[pl.ds(side * groups + 2 * k, 2)]
        return pltpu.make_async_remote_copy(
            src_ref=rows,
            dst_ref=rows,
            send_sem=n_send.at[k],
            recv_sem=n_recv.at[k],
            device_id=(engine, z, other),
            device_id_type=MESH,
        )

    def own(m):
        g = engine * n_f + z
        copy(m, g, CROSS).start()

        @pl.when(z > 0)
        def _():
            copy(m, g, LEFT).start()

        @pl.when(z < n_f - 1)
        def _():
            copy(m, g, RIGHT).start()

        copy(m, g, SIB).start()

    last = n_f - 1

    def at_end(zz):
        return (zz == 0) | (zz == last)

    def relay_cross(m, g, zz):
        if m == KV:
            pl.when((zz > 0) & (zz < last))(lambda: copy(m, g, CROSS).start())
        else:
            copy(m, g, CROSS).start()

    def along(m, d):
        @pl.when(z >= d)
        def _():
            g = engine * n_f + z - d
            copy(m, g, SIB).wait_recv()

            @pl.when(z < n_f - 1)
            def _():
                copy(m, g, RIGHT).start()

            relay_cross(m, g, z - d)
            copy(m, g, SIB).start()

        @pl.when(z + d < n_f)
        def _():
            g = engine * n_f + z + d
            copy(m, g, SIB).wait_recv()

            @pl.when(z > 0)
            def _():
                copy(m, g, LEFT).start()

            relay_cross(m, g, z + d)
            copy(m, g, SIB).start()

    def far(m):
        @pl.when(z > 0)
        def _():
            g = across * n_f
            copy(m, g, SIB).wait_recv()
            pl.when(z < last)(lambda: copy(m, g, RIGHT).start())
            copy(m, g, SIB).start()

        @pl.when(z < last)
        def _():
            g = across * n_f + last
            copy(m, g, SIB).wait_recv()
            pl.when(z > 0)(lambda: copy(m, g, LEFT).start())
            copy(m, g, SIB).start()

    def crossing(m, d):
        def take(zz):
            g = across * n_f + zz
            copy(m, g, SIB).wait_recv()
            copy(m, g, SIB).start()

        def late(zz):
            return (zz > 0) & (zz < last) if m == KV else zz >= 0

        if d == 0:
            take(z)
            if m == KV:
                g = across * n_f + z
                pl.when(z == 0)(lambda: copy(m, g, RIGHT).start())
                pl.when(z == last)(lambda: copy(m, g, LEFT).start())
        else:
            pl.when((z >= d) & late(z - d))(lambda: take(z - d))
            pl.when((z + d < n_f) & late(z + d))(lambda: take(z + d))

    def from_sibling(m):
        def arrived(k, carry):
            copy(m, sibling * n_f + k, SIB).wait_recv()
            copy(m, lax.rem(sibling + 2, 4) * n_f + k, SIB).wait_recv()
            return carry

        lax.fori_loop(0, n_f, arrived, 0)

    loads = [
        pltpu.make_async_copy(source, target, load_sem.at[k])
        for k, (source, target) in enumerate(
            (
                (kvbase_hbm, kv_buf.at[mine]),
                (odown_hbm, odown_ref),
                (input_hbm, input_ref),
                (qbase_hbm, qbase_ref),
                (qdown_hbm, qdown_ref),
                (qup_hbm, qup_ref),
                (gain_hbm, gain_ref),
                (obase_hbm, obase_ref),
                (oup_hbm, oup_ref),
                (places_hbm, places_ref),
                (ckeys_hbm, ckeys_ref),
                (cvalues_hbm, cvalues_ref),
            )
        )
    ]
    for load in loads:
        load.start()

    barrier = pltpu.get_barrier_semaphore()

    def greet(target):
        pl.semaphore_signal(barrier, inc=1, device_id=target, device_id_type=MESH)

    greet((sibling, z, t))
    greet((across, z, t))
    greet((engine, z, other))
    pl.when(z > 0)(lambda: greet((engine, z - 1, t)))
    pl.when(z < n_f - 1)(lambda: greet((engine, z + 1, t)))

    loads[0].wait()
    loads[1].wait()
    down_full[t] = odown_ref[...]
    pl.semaphore_wait(barrier, 5 - (z == 0).astype(jnp.int32) - (z == n_f - 1).astype(jnp.int32))

    own(KV)
    to_partner(down_full, 1).start()
    loads[2].wait()
    total = jnp.zeros((tok, 128), jnp.float32)
    for k in range(input_ref.shape[1] // 128):
        wide = input_ref[:, k * 128 : (k + 1) * 128].astype(jnp.float32)
        total = total + wide * wide
    squares[t] = total
    to_partner(squares, 0).start()

    over_rank = (((0,), (0,)), ((), ()))
    for k in range(3, 6):
        loads[k].wait()
    q_buf[mine] = (
        qbase_ref[...].astype(jnp.float32)
        + 2.0
        * lax.dot_general(
            qdown_ref[...], qup_ref[...], over_rank, preferred_element_type=jnp.float32
        )
    ).astype(jnp.bfloat16)
    own(QUERY)

    loads[6].wait()
    from_partner(squares, 0).wait_recv()
    mean = jnp.sum(squares[0] + squares[1], axis=1, keepdims=True) * (1.0 / width)
    scale = jnp.broadcast_to(lax.rsqrt(mean + 1e-05), (tok, 128))
    each = piece // 128
    for k in range(groups):
        for part in range(each):
            at = k * each + part
            normed[t * groups + k, :, part * 128 : (part + 1) * 128] = (
                input_ref[:, at * 128 : (at + 1) * 128].astype(jnp.float32)
                * scale
                * gain_ref[at : at + 1, :].astype(jnp.float32)
            ).astype(jnp.bfloat16)
        if k % 2 == 1:
            normed_copy(t, k // 2).start()

    for k in range(7, len(loads)):
        loads[k].wait()

    along(KV, 1)
    crossing(KV, 0)
    along(KV, 2)
    far(KV)

    from_partner(down_full, 1).wait_recv()
    for side in range(2):
        rows = slice(side * head, (side + 1) * head)
        o_buf[mine, rows, :] = (
            obase_ref[rows, :].astype(jnp.float32)
            + 2.0
            * lax.dot_general(
                down_full[side], oup_ref[...], over_rank, preferred_element_type=jnp.float32
            )
        ).astype(jnp.bfloat16)
    along(QUERY, 1)
    along(KV, 3)

    lane = lax.broadcasted_iota(jnp.int32, (tok, head), 1)
    low = lane < head // 2
    index = jnp.where(low, lane, lane - head // 2).astype(jnp.float32)
    inverse = jnp.exp(index * (-2.0 / head) * jnp.log(jnp.full((tok, head), 500000.0, jnp.float32)))
    places = jnp.broadcast_to(places_ref[...].astype(jnp.float32), (head, tok)).T
    angle = places * inverse
    cosine_ref[...] = jnp.cos(angle)
    sine_ref[...] = jnp.where(low, -jnp.sin(angle), jnp.sin(angle))

    def rope(values):
        return values * cosine_ref[...] + pltpu.roll(values, head // 2, 1) * sine_ref[...]

    along(QUERY, 2)
    own(OUT)
    crossing(KV, 1)
    along(QUERY, 3)
    crossing(KV, 2)
    along(OUT, 1)
    crossing(KV, 3)
    crossing(QUERY, 0)
    along(OUT, 2)
    from_sibling(KV)
    kv_part[t] = jnp.zeros(kv_part.shape[1:], jnp.float32)

    def kv_step(g, carry):
        kv_part[t] += jnp.dot(
            normed[t * groups + g], kv_buf[g], preferred_element_type=jnp.float32
        )
        return carry

    lax.fori_loop(0, groups // 2, kv_step, 0)
    crossing(QUERY, 1)
    along(OUT, 3)
    lax.fori_loop(groups // 2, groups, kv_step, 0)
    to_partner(kv_part, 2).start()
    crossing(QUERY, 2)
    crossing(QUERY, 3)
    crossing(OUT, 0)

    from_sibling(QUERY)
    q_total[...] = jnp.zeros_like(q_total)

    def q_step(g):
        q_total[...] += jnp.dot(
            normed[2 * g], q_buf[g, :piece, :], preferred_element_type=jnp.float32
        ) + jnp.dot(normed[2 * g + 1], q_buf[g, piece:, :], preferred_element_type=jnp.float32)

    def q_near(k, carry):
        q_step(t * half_groups + k)
        return carry

    def q_far(k, carry):
        normed_copy(other, k).wait_recv()
        q_step(other * half_groups + k)
        return carry

    lax.fori_loop(0, half_groups, q_near, 0)
    crossing(OUT, 1)
    lax.fori_loop(0, half_groups, q_far, 0)

    query = rope(q_total[...]).astype(jnp.bfloat16)
    from_partner(kv_part, 2).wait_recv()
    kv = kv_part[0] + kv_part[1]
    new_keys = rope(kv[:, :head]).astype(jnp.bfloat16)
    new_values = kv[:, head:].astype(jnp.bfloat16)
    dims = (((1,), (1,)), ((), ()))
    slots = ckeys_ref.shape[0]
    factor = head ** (-0.5)
    old = lax.dot_general(query, ckeys_ref[...], dims, preferred_element_type=jnp.float32) * factor
    new = lax.dot_general(query, new_keys, dims, preferred_element_type=jnp.float32) * factor
    seen = lax.broadcasted_iota(jnp.int32, (tok, slots), 1) < offset_ref[0]
    rows = lax.broadcasted_iota(jnp.int32, (tok, tok), 0)
    columns = lax.broadcasted_iota(jnp.int32, (tok, tok), 1)
    old = jnp.where(seen, old, jnp.float32(-1e30))
    new = jnp.where(columns <= rows, new, jnp.float32(-1e30))
    top = jnp.maximum(
        jnp.max(old, axis=1, keepdims=True), jnp.max(new, axis=1, keepdims=True)
    )
    old = jnp.exp(old - top)
    new = jnp.exp(new - top)
    summed = jnp.sum(old, axis=1, keepdims=True) + jnp.sum(new, axis=1, keepdims=True)
    old = (old / summed).astype(jnp.bfloat16)
    new = (new / summed).astype(jnp.bfloat16)
    own_head = (
        jnp.dot(old, cvalues_ref[...], preferred_element_type=jnp.float32)
        + jnp.dot(new, new_values, preferred_element_type=jnp.float32)
    ).astype(jnp.bfloat16)
    heads[t] = own_head
    to_partner(heads, 3).start()
    from_partner(heads, 3).wait_recv()

    both[:, :head] = heads[0]
    both[:, head:] = heads[1]

    def project(g):
        result_ref[:, pl.ds(pl.multiple_of(g * piece, piece), piece)] = jnp.dot(
            both[...], o_buf[g], preferred_element_type=jnp.float32
        ).astype(jnp.bfloat16)

    def near(k, carry):
        project(engine * n_f + k)
        g = sibling * n_f + k
        copy(OUT, g, SIB).wait_recv()
        project(g)
        return carry

    def crossed(d):
        def pair(zz):
            project(across * n_f + zz)
            g = lax.rem(sibling + 2, 4) * n_f + zz
            copy(OUT, g, SIB).wait_recv()
            project(g)

        if d == 0:
            pair(z)
        else:
            pl.when(z >= d)(lambda: pair(z - d))
            pl.when(z + d < n_f)(lambda: pair(z + d))

    lax.fori_loop(0, n_f, near, 0)
    crossing(OUT, 2)
    crossed(0)
    crossed(1)
    crossing(OUT, 3)
    crossed(2)
    crossed(3)

    for m in range(3):

        def drain(k, carry, m=m):
            g = engine * n_f + k
            copy(m, g, SIB).wait_send()
            far_g = across * n_f + k
            copy(m, far_g, SIB).wait_send()
            if m == KV:
                pl.when(~at_end(k) | (k == z))(lambda: copy(m, g, CROSS).wait_send())
                pl.when((k == 0) & (z < last))(lambda: copy(m, far_g, RIGHT).wait_send())
                pl.when((k == last) & (z > 0))(lambda: copy(m, far_g, LEFT).wait_send())
            else:
                copy(m, g, CROSS).wait_send()

            @pl.when((z > 0) & (k >= z))
            def _():
                copy(m, g, LEFT).wait_send()

            @pl.when((z < n_f - 1) & (k <= z))
            def _():
                copy(m, g, RIGHT).wait_send()

            return carry

        lax.fori_loop(0, n_f, drain, 0)

    def drain_normed(k, carry):
        normed_copy(t, k).wait_send()
        return carry

    lax.fori_loop(0, half_groups, drain_normed, 0)
    to_partner(squares, 0).wait_send()
    to_partner(down_full, 1).wait_send()
    to_partner(kv_part, 2).wait_send()
    to_partner(heads, 3).wait_send()


def per_device(
    n_f,
    layer_input,
    norm_gain,
    query_base,
    query_down,
    query_up,
    kv_base,
    output_base_weight,
    output_down_factor,
    output_up_factor,
    cache_keys,
    cache_values,
    positions,
    offsets,
):
    tok, features = layer_input.shape
    depth, head = query_base.shape
    rank = query_up.shape[0]
    groups = 4 * n_f
    kv_base = kv_base[0]
    output_base_weight = output_base_weight[:, 0]
    output_up_factor = output_up_factor[:, 0]
    piece = kv_base.shape[0]
    vmem = pl.BlockSpec(memory_space=pltpu.VMEM)
    hbm = pl.BlockSpec(memory_space=pltpu.HBM)
    smem = pl.BlockSpec(memory_space=pltpu.SMEM)
    dma = pltpu.SemaphoreType.DMA
    return pl.pallas_call(
        functools.partial(kernel, n_f),
        out_shape=jax.ShapeDtypeStruct((tok, features), jnp.bfloat16),
        in_specs=[hbm] * 12 + [smem],
        out_specs=vmem,
        scratch_shapes=[
            pltpu.VMEM((tok, features), jnp.bfloat16),
            pltpu.VMEM((features // 128, 128), jnp.bfloat16),
            pltpu.VMEM(query_base.shape, jnp.bfloat16),
            pltpu.VMEM((rank, depth), jnp.bfloat16),
            pltpu.VMEM(query_up.shape, jnp.bfloat16),
            pltpu.VMEM(output_base_weight.shape, jnp.bfloat16),
            pltpu.VMEM((rank, head), jnp.bfloat16),
            pltpu.VMEM(output_up_factor.shape, jnp.bfloat16),
            pltpu.VMEM(cache_keys.shape[1:], jnp.bfloat16),
            pltpu.VMEM(cache_values.shape[1:], jnp.bfloat16),
            pltpu.VMEM(positions.shape, jnp.int32),
            pltpu.VMEM((groups,) + kv_base.shape, jnp.bfloat16),
            pltpu.VMEM((groups,) + query_base.shape, jnp.bfloat16),
            pltpu.VMEM((groups,) + output_base_weight.shape, jnp.bfloat16),
            pltpu.VMEM((2 * groups, tok, piece), jnp.bfloat16),
            pltpu.VMEM((2, tok, 128), jnp.float32),
            pltpu.VMEM((2, rank, head), jnp.bfloat16),
            pltpu.VMEM((2, tok, 2 * head), jnp.float32),
            pltpu.VMEM((tok, head), jnp.float32),
            pltpu.VMEM((2, tok, head), jnp.bfloat16),
            pltpu.VMEM((tok, 2 * head), jnp.bfloat16),
            pltpu.VMEM((tok, head), jnp.float32),
            pltpu.VMEM((tok, head), jnp.float32),
            dma((3, groups)),
            dma((3, 4, groups)),
            dma((4,)),
            dma((4,)),
            dma((groups // 2,)),
            dma((groups // 2,)),
            dma((12,)),
        ],
        compiler_params=pltpu.CompilerParams(
            collective_id=0, has_side_effects=True, vmem_limit_bytes=60 * 1024 * 1024
        ),
    )(
        layer_input,
        norm_gain.reshape(-1, 128),
        query_base,
        query_down.T,
        query_up,
        kv_base,
        output_base_weight,
        output_down_factor.T,
        output_up_factor,
        cache_keys[0],
        cache_values[0],
        positions,
        offsets,
    )


def solution(mesh):
    in_specs = (
        P(("engine", "fsdp"), "tensor"),
        P("tensor"),
        P(("engine", "fsdp"), "tensor"),
        P(("engine", "fsdp"), None),
        P(None, "tensor"),
        P("tensor", ("engine", "fsdp"), None),
        P(None, "tensor", ("engine", "fsdp")),
        P("tensor", None),
        P(None, "tensor", ("engine", "fsdp")),
        P(("engine", "fsdp"), None, None),
        P(("engine", "fsdp"), None, None),
        P(("engine", "fsdp"), None),
        P(("engine", "fsdp")),
    )
    out_specs = P(("engine", "fsdp"), "tensor")
    shape = dict(mesh.shape)
    paired = shape["tensor"] == 2 and shape["engine"] == 4
    body = functools.partial(per_device, shape["fsdp"]) if paired else per_device_plain
    return jax.shard_map(
        body, mesh=mesh, in_specs=in_specs, out_specs=out_specs, check_vma=False
    )
```

```python
import functools

import jax
import jax.numpy as jnp
from jax import lax
from jax.experimental import pallas as pl
from jax.experimental.pallas import tpu as pltpu
from jax.sharding import PartitionSpec as P

MESH = pl.DeviceIdType.MESH
KV, QUERY, OUT = 0, 1, 2
SIB, CROSS, LEFT, RIGHT = 0, 1, 2, 3


def rotate(values, places):
    half = values.shape[-1] // 2
    index = jnp.arange(half).astype(jnp.float32)
    inverse = jnp.exp(index * (-2.0 / values.shape[-1]) * jnp.log(jnp.float32(500000.0)))
    angle = places.astype(jnp.float32)[:, None] * inverse[None, :]
    cosine = jnp.cos(angle)
    sine = jnp.sin(angle)
    first = values[:, :half]
    second = values[:, half:]
    return jnp.concatenate([first * cosine - second * sine, second * cosine + first * sine], axis=1)


def attend(query, new_keys, new_values, old_keys, old_values, offset):
    tok_count = query.shape[0]
    slots = old_keys.shape[0]
    keys_all = jnp.concatenate([old_keys, new_keys], axis=0)
    values_all = jnp.concatenate([old_values, new_values], axis=0)
    scores = jnp.dot(query, keys_all.T, preferred_element_type=jnp.float32) * query.shape[-1] ** (
        -0.5
    )
    slot_seen = jnp.broadcast_to(jnp.arange(slots)[None, :] < offset, (tok_count, slots))
    rows = jnp.arange(tok_count)
    new_seen = rows[None, :] <= rows[:, None]
    seen = jnp.concatenate([slot_seen, new_seen], axis=1)
    scores = jnp.where(seen, scores, jnp.float32(-1e30))
    top = jnp.max(scores, axis=1, keepdims=True)
    probs = jnp.exp(scores - top)
    weights = (probs / jnp.sum(probs, axis=1, keepdims=True)).astype(jnp.bfloat16)
    return jnp.dot(weights, values_all, preferred_element_type=jnp.float32).astype(jnp.bfloat16)


def per_device_plain(
    layer_input,
    norm_gain,
    query_base,
    query_down,
    query_up,
    kv_base,
    output_base_weight,
    output_down_factor,
    output_up_factor,
    cache_keys,
    cache_values,
    positions,
    offsets,
):
    head_size = query_base.shape[1]
    tok_count = layer_input.shape[0]
    full_input, full_gain, complete_down_factor = (
        lax.all_gather(layer_input, "tensor", axis=1, tiled=True),
        lax.all_gather(norm_gain, "tensor", axis=0, tiled=True),
        lax.all_gather(output_down_factor, "tensor", axis=0, tiled=True),
    )
    wide = full_input.astype(jnp.float32)
    scale = lax.rsqrt(jnp.mean(wide * wide, axis=1, keepdims=True) + 1e-05)
    normed = (wide * scale * full_gain.astype(jnp.float32)[None, :]).astype(jnp.bfloat16)
    local_normed = (
        layer_input.astype(jnp.float32) * scale * norm_gain.astype(jnp.float32)[None, :]
    ).astype(jnp.bfloat16)
    merged_query = (
        query_base.astype(jnp.float32)
        + 2.0 * jnp.dot(query_down, query_up, preferred_element_type=jnp.float32)
    ).astype(jnp.bfloat16)
    columns = normed
    query_raw = jnp.dot(
        columns,
        lax.all_gather(merged_query, ("engine", "fsdp"), axis=0, tiled=True),
        preferred_element_type=jnp.float32,
    )
    columns = local_normed
    kv_part = jnp.dot(
        columns,
        lax.all_gather(kv_base, ("engine", "fsdp"), axis=1, tiled=True)[0],
        preferred_element_type=jnp.float32,
    )
    kv_total = lax.psum(kv_part.astype(jnp.bfloat16), "tensor").astype(jnp.float32)
    places = positions[0]
    query = rotate(query_raw, places).astype(jnp.bfloat16)
    new_keys = rotate(kv_total[:, :head_size], places).astype(jnp.bfloat16)
    new_values = kv_total[:, head_size:].astype(jnp.bfloat16)
    head_out = attend(query, new_keys, new_values, cache_keys[0], cache_values[0], offsets[0])
    adapter_output_delta = jnp.einsum(
        "lz,zam->lam",
        complete_down_factor.astype(jnp.float32),
        output_up_factor.astype(jnp.float32),
    )
    combined_output_weight = (
        output_base_weight.astype(jnp.float32) + 2.0 * adapter_output_delta
    ).astype(jnp.bfloat16)
    own_rows = lax.all_to_all(
        combined_output_weight, "tensor", split_axis=0, concat_axis=1, tiled=True
    )
    terms = jnp.einsum(
        "tk,kbn->tbn",
        head_out,
        lax.all_gather(own_rows, ("engine", "fsdp"), axis=2, tiled=True),
        preferred_element_type=jnp.float32,
    )
    flat_terms = terms.reshape(tok_count, terms.shape[1] * terms.shape[2])
    attended = lax.psum_scatter(
        flat_terms.astype(jnp.bfloat16), "tensor", scatter_dimension=1, tiled=True
    )
    return attended


def kernel(
    n_f,
    input_hbm,
    gain_hbm,
    qbase_hbm,
    qdown_hbm,
    qup_hbm,
    kvbase_hbm,
    obase_hbm,
    odown_hbm,
    oup_hbm,
    ckeys_hbm,
    cvalues_hbm,
    places_hbm,
    offset_ref,
    result_ref,
    input_ref,
    gain_ref,
    qbase_ref,
    qdown_ref,
    qup_ref,
    obase_ref,
    odown_ref,
    oup_ref,
    ckeys_ref,
    cvalues_ref,
    places_ref,
    kv_buf,
    q_buf,
    o_buf,
    normed,
    squares,
    down_full,
    kv_part,
    q_total,
    heads,
    both,
    cosine_ref,
    sine_ref,
    recv_sem,
    send_sem,
    y_recv,
    y_send,
    n_recv,
    n_send,
    load_sem,
):
    engine = lax.axis_index("engine")
    z = lax.axis_index("fsdp")
    t = lax.axis_index("tensor")
    core = lax.rem(engine, 2)
    sibling = engine + 1 - 2 * core
    across = lax.rem(engine + 2, 4)
    other = 1 - t
    bufs = (kv_buf, q_buf, o_buf)
    groups = 4 * n_f
    tok = input_ref.shape[0]
    head = qbase_ref.shape[1]
    piece = kvbase_hbm.shape[0]
    half_groups = groups // 2
    mine = engine * n_f + z
    width = 2 * input_ref.shape[1]

    def copy(m, g, way):
        target = {
            SIB: (sibling, z, t),
            CROSS: (across, z, t),
            LEFT: (engine, jnp.maximum(z - 1, 0), t),
            RIGHT: (engine, jnp.minimum(z + 1, n_f - 1), t),
        }[way]
        return pltpu.make_async_remote_copy(
            src_ref=bufs[m].at[g],
            dst_ref=bufs[m].at[g],
            send_sem=send_sem.at[m, way, g],
            recv_sem=recv_sem.at[m, g],
            device_id=target,
            device_id_type=MESH,
        )

    def to_partner(ref, k):
        return pltpu.make_async_remote_copy(
            src_ref=ref.at[t],
            dst_ref=ref.at[t],
            send_sem=y_send.at[k],
            recv_sem=y_recv.at[k],
            device_id=(engine, z, other),
            device_id_type=MESH,
        )

    def from_partner(ref, k):
        return pltpu.make_async_remote_copy(
            src_ref=ref.at[other],
            dst_ref=ref.at[other],
            send_sem=y_send.at[k],
            recv_sem=y_recv.at[k],
            device_id=(engine, z, other),
            device_id_type=MESH,
        )

    def normed_copy(side, k):
        rows = normed.at[pl.ds(side * groups + 2 * k, 2)]
        return pltpu.make_async_remote_copy(
            src_ref=rows,
            dst_ref=rows,
            send_sem=n_send.at[k],
            recv_sem=n_recv.at[k],
            device_id=(engine, z, other),
            device_id_type=MESH,
        )

    def own(m):
        g = engine * n_f + z
        copy(m, g, CROSS).start()

        @pl.when(z > 0)
        def _():
            copy(m, g, LEFT).start()

        @pl.when(z < n_f - 1)
        def _():
            copy(m, g, RIGHT).start()

        copy(m, g, SIB).start()

    def along(m, d):
        @pl.when(z >= d)
        def _():
            g = engine * n_f + z - d
            copy(m, g, SIB).wait_recv()

            @pl.when(z < n_f - 1)
            def _():
                copy(m, g, RIGHT).start()

            copy(m, g, CROSS).start()
            copy(m, g, SIB).start()

        @pl.when(z + d < n_f)
        def _():
            g = engine * n_f + z + d
            copy(m, g, SIB).wait_recv()

            @pl.when(z > 0)
            def _():
                copy(m, g, LEFT).start()

            copy(m, g, CROSS).start()
            copy(m, g, SIB).start()

    def crossing(m, d):
        def take(zz):
            g = across * n_f + zz
            copy(m, g, SIB).wait_recv()
            copy(m, g, SIB).start()

        if d == 0:
            take(z)
        else:
            pl.when(z >= d)(lambda: take(z - d))
            pl.when(z + d < n_f)(lambda: take(z + d))

    def from_sibling(m):
        def arrived(k, carry):
            copy(m, sibling * n_f + k, SIB).wait_recv()
            copy(m, lax.rem(sibling + 2, 4) * n_f + k, SIB).wait_recv()
            return carry

        lax.fori_loop(0, n_f, arrived, 0)

    loads = [
        pltpu.make_async_copy(source, target, load_sem.at[k])
        for k, (source, target) in enumerate(
            (
                (kvbase_hbm, kv_buf.at[mine]),
                (odown_hbm, odown_ref),
                (input_hbm, input_ref),
                (qbase_hbm, qbase_ref),
                (qdown_hbm, qdown_ref),
                (qup_hbm, qup_ref),
                (gain_hbm, gain_ref),
                (obase_hbm, obase_ref),
                (oup_hbm, oup_ref),
                (places_hbm, places_ref),
                (ckeys_hbm, ckeys_ref),
                (cvalues_hbm, cvalues_ref),
            )
        )
    ]
    for load in loads:
        load.start()

    barrier = pltpu.get_barrier_semaphore()

    def greet(target):
        pl.semaphore_signal(barrier, inc=1, device_id=target, device_id_type=MESH)

    greet((sibling, z, t))
    greet((across, z, t))
    greet((engine, z, other))
    pl.when(z > 0)(lambda: greet((engine, z - 1, t)))
    pl.when(z < n_f - 1)(lambda: greet((engine, z + 1, t)))

    loads[0].wait()
    loads[1].wait()
    down_full[t] = odown_ref[...]
    pl.semaphore_wait(barrier, 5 - (z == 0).astype(jnp.int32) - (z == n_f - 1).astype(jnp.int32))

    own(KV)
    to_partner(down_full, 1).start()
    loads[2].wait()
    total = jnp.zeros((tok, 128), jnp.float32)
    for k in range(input_ref.shape[1] // 128):
        wide = input_ref[:, k * 128 : (k + 1) * 128].astype(jnp.float32)
        total = total + wide * wide
    squares[t] = total
    to_partner(squares, 0).start()

    over_rank = (((0,), (0,)), ((), ()))
    for k in range(3, 6):
        loads[k].wait()
    q_buf[mine] = (
        qbase_ref[...].astype(jnp.float32)
        + 2.0
        * lax.dot_general(
            qdown_ref[...], qup_ref[...], over_rank, preferred_element_type=jnp.float32
        )
    ).astype(jnp.bfloat16)
    own(QUERY)

    loads[6].wait()
    from_partner(squares, 0).wait_recv()
    mean = jnp.sum(squares[0] + squares[1], axis=1, keepdims=True) * (1.0 / width)
    scale = jnp.broadcast_to(lax.rsqrt(mean + 1e-05), (tok, 128))
    each = piece // 128
    for k in range(groups):
        for part in range(each):
            at = k * each + part
            normed[t * groups + k, :, part * 128 : (part + 1) * 128] = (
                input_ref[:, at * 128 : (at + 1) * 128].astype(jnp.float32)
                * scale
                * gain_ref[at : at + 1, :].astype(jnp.float32)
            ).astype(jnp.bfloat16)
        if k % 2 == 1:
            normed_copy(t, k // 2).start()

    for k in range(7, len(loads)):
        loads[k].wait()

    along(KV, 1)
    along(KV, 2)

    from_partner(down_full, 1).wait_recv()
    for side in range(2):
        rows = slice(side * head, (side + 1) * head)
        o_buf[mine, rows, :] = (
            obase_ref[rows, :].astype(jnp.float32)
            + 2.0
            * lax.dot_general(
                down_full[side], oup_ref[...], over_rank, preferred_element_type=jnp.float32
            )
        ).astype(jnp.bfloat16)
    own(OUT)

    along(QUERY, 1)
    along(KV, 3)
    crossing(KV, 0)

    lane = lax.broadcasted_iota(jnp.int32, (tok, head), 1)
    low = lane < head // 2
    index = jnp.where(low, lane, lane - head // 2).astype(jnp.float32)
    inverse = jnp.exp(index * (-2.0 / head) * jnp.log(jnp.full((tok, head), 500000.0, jnp.float32)))
    places = jnp.broadcast_to(places_ref[...].astype(jnp.float32), (head, tok)).T
    angle = places * inverse
    cosine_ref[...] = jnp.cos(angle)
    sine_ref[...] = jnp.where(low, -jnp.sin(angle), jnp.sin(angle))

    def rope(values):
        return values * cosine_ref[...] + pltpu.roll(values, head // 2, 1) * sine_ref[...]

    along(QUERY, 2)
    crossing(KV, 1)
    along(QUERY, 3)
    crossing(KV, 2)
    along(OUT, 1)
    crossing(KV, 3)
    crossing(QUERY, 0)
    along(OUT, 2)
    from_sibling(KV)
    kv_part[t] = jnp.zeros(kv_part.shape[1:], jnp.float32)

    def kv_step(g, carry):
        kv_part[t] += jnp.dot(
            normed[t * groups + g], kv_buf[g], preferred_element_type=jnp.float32
        )
        return carry

    lax.fori_loop(0, groups // 2, kv_step, 0)
    crossing(QUERY, 1)
    along(OUT, 3)
    lax.fori_loop(groups // 2, groups, kv_step, 0)
    to_partner(kv_part, 2).start()

    q_total[...] = jnp.zeros_like(q_total)
    local = engine // 2 == t

    def q_step(g):
        @pl.when(g // half_groups != t)
        def _():
            normed_copy(other, lax.rem(g, half_groups)).wait_recv()

        q_total[...] += jnp.dot(
            normed[2 * g], q_buf[g, :piece, :], preferred_element_type=jnp.float32
        ) + jnp.dot(normed[2 * g + 1], q_buf[g, piece:, :], preferred_element_type=jnp.float32)

    def q_column():
        def step(k, carry):
            q_step(engine * n_f + k)
            g = sibling * n_f + k
            copy(QUERY, g, SIB).wait_recv()
            q_step(g)
            return carry

        lax.fori_loop(0, n_f, step, 0)

    def q_crossed(d):
        def pair(zz):
            q_step(across * n_f + zz)
            g = lax.rem(sibling + 2, 4) * n_f + zz
            copy(QUERY, g, SIB).wait_recv()
            q_step(g)

        if d == 0:
            pair(z)
        else:
            pl.when(z >= d)(lambda: pair(z - d))
            pl.when(z + d < n_f)(lambda: pair(z + d))

    def q_first():
        q_crossed(0)
        q_crossed(1)

    pl.when(local)(q_column)
    pl.when(jnp.logical_not(local))(q_first)
    crossing(QUERY, 2)
    pl.when(local)(q_first)
    pl.when(jnp.logical_not(local))(q_column)
    crossing(QUERY, 3)
    crossing(OUT, 0)
    q_crossed(2)
    q_crossed(3)

    query = rope(q_total[...]).astype(jnp.bfloat16)
    from_partner(kv_part, 2).wait_recv()
    kv = kv_part[0] + kv_part[1]
    new_keys = rope(kv[:, :head]).astype(jnp.bfloat16)
    new_values = kv[:, head:].astype(jnp.bfloat16)
    dims = (((1,), (1,)), ((), ()))
    slots = ckeys_ref.shape[0]
    factor = head ** (-0.5)
    old = lax.dot_general(query, ckeys_ref[...], dims, preferred_element_type=jnp.float32) * factor
    new = lax.dot_general(query, new_keys, dims, preferred_element_type=jnp.float32) * factor
    seen = lax.broadcasted_iota(jnp.int32, (tok, slots), 1) < offset_ref[0]
    rows = lax.broadcasted_iota(jnp.int32, (tok, tok), 0)
    columns = lax.broadcasted_iota(jnp.int32, (tok, tok), 1)
    old = jnp.where(seen, old, jnp.float32(-1e30))
    new = jnp.where(columns <= rows, new, jnp.float32(-1e30))
    top = jnp.maximum(
        jnp.max(old, axis=1, keepdims=True), jnp.max(new, axis=1, keepdims=True)
    )
    old = jnp.exp(old - top)
    new = jnp.exp(new - top)
    summed = jnp.sum(old, axis=1, keepdims=True) + jnp.sum(new, axis=1, keepdims=True)
    old = (old / summed).astype(jnp.bfloat16)
    new = (new / summed).astype(jnp.bfloat16)
    own_head = (
        jnp.dot(old, cvalues_ref[...], preferred_element_type=jnp.float32)
        + jnp.dot(new, new_values, preferred_element_type=jnp.float32)
    ).astype(jnp.bfloat16)
    heads[t] = own_head
    to_partner(heads, 3).start()
    crossing(OUT, 1)
    from_partner(heads, 3).wait_recv()

    both[:, :head] = heads[0]
    both[:, head:] = heads[1]

    def project(g):
        result_ref[:, pl.ds(pl.multiple_of(g * piece, piece), piece)] = jnp.dot(
            both[...], o_buf[g], preferred_element_type=jnp.float32
        ).astype(jnp.bfloat16)

    def near(k, carry):
        project(engine * n_f + k)
        g = sibling * n_f + k
        copy(OUT, g, SIB).wait_recv()
        project(g)
        return carry

    def crossed(d):
        def pair(zz):
            project(across * n_f + zz)
            g = lax.rem(sibling + 2, 4) * n_f + zz
            copy(OUT, g, SIB).wait_recv()
            project(g)

        if d == 0:
            pair(z)
        else:
            pl.when(z >= d)(lambda: pair(z - d))
            pl.when(z + d < n_f)(lambda: pair(z + d))

    lax.fori_loop(0, n_f, near, 0)
    crossing(OUT, 2)
    crossed(0)
    crossed(1)
    crossing(OUT, 3)
    crossed(2)
    crossed(3)

    for m in range(3):

        def drain(k, carry, m=m):
            g = engine * n_f + k
            copy(m, g, SIB).wait_send()
            copy(m, g, CROSS).wait_send()
            copy(m, across * n_f + k, SIB).wait_send()

            @pl.when((z > 0) & (k >= z))
            def _():
                copy(m, g, LEFT).wait_send()

            @pl.when((z < n_f - 1) & (k <= z))
            def _():
                copy(m, g, RIGHT).wait_send()

            return carry

        lax.fori_loop(0, n_f, drain, 0)

    def drain_normed(k, carry):
        normed_copy(t, k).wait_send()
        return carry

    lax.fori_loop(0, half_groups, drain_normed, 0)
    to_partner(squares, 0).wait_send()
    to_partner(down_full, 1).wait_send()
    to_partner(kv_part, 2).wait_send()
    to_partner(heads, 3).wait_send()


def per_device(
    n_f,
    layer_input,
    norm_gain,
    query_base,
    query_down,
    query_up,
    kv_base,
    output_base_weight,
    output_down_factor,
    output_up_factor,
    cache_keys,
    cache_values,
    positions,
    offsets,
):
    tok, features = layer_input.shape
    depth, head = query_base.shape
    rank = query_up.shape[0]
    groups = 4 * n_f
    kv_base = kv_base[0]
    output_base_weight = output_base_weight[:, 0]
    output_up_factor = output_up_factor[:, 0]
    piece = kv_base.shape[0]
    vmem = pl.BlockSpec(memory_space=pltpu.VMEM)
    hbm = pl.BlockSpec(memory_space=pltpu.HBM)
    smem = pl.BlockSpec(memory_space=pltpu.SMEM)
    dma = pltpu.SemaphoreType.DMA
    return pl.pallas_call(
        functools.partial(kernel, n_f),
        out_shape=jax.ShapeDtypeStruct((tok, features), jnp.bfloat16),
        in_specs=[hbm] * 12 + [smem],
        out_specs=vmem,
        scratch_shapes=[
            pltpu.VMEM((tok, features), jnp.bfloat16),
            pltpu.VMEM((features // 128, 128), jnp.bfloat16),
            pltpu.VMEM(query_base.shape, jnp.bfloat16),
            pltpu.VMEM((rank, depth), jnp.bfloat16),
            pltpu.VMEM(query_up.shape, jnp.bfloat16),
            pltpu.VMEM(output_base_weight.shape, jnp.bfloat16),
            pltpu.VMEM((rank, head), jnp.bfloat16),
            pltpu.VMEM(output_up_factor.shape, jnp.bfloat16),
            pltpu.VMEM(cache_keys.shape[1:], jnp.bfloat16),
            pltpu.VMEM(cache_values.shape[1:], jnp.bfloat16),
            pltpu.VMEM(positions.shape, jnp.int32),
            pltpu.VMEM((groups,) + kv_base.shape, jnp.bfloat16),
            pltpu.VMEM((groups,) + query_base.shape, jnp.bfloat16),
            pltpu.VMEM((groups,) + output_base_weight.shape, jnp.bfloat16),
            pltpu.VMEM((2 * groups, tok, piece), jnp.bfloat16),
            pltpu.VMEM((2, tok, 128), jnp.float32),
            pltpu.VMEM((2, rank, head), jnp.bfloat16),
            pltpu.VMEM((2, tok, 2 * head), jnp.float32),
            pltpu.VMEM((tok, head), jnp.float32),
            pltpu.VMEM((2, tok, head), jnp.bfloat16),
            pltpu.VMEM((tok, 2 * head), jnp.bfloat16),
            pltpu.VMEM((tok, head), jnp.float32),
            pltpu.VMEM((tok, head), jnp.float32),
            dma((3, groups)),
            dma((3, 4, groups)),
            dma((4,)),
            dma((4,)),
            dma((groups // 2,)),
            dma((groups // 2,)),
            dma((12,)),
        ],
        compiler_params=pltpu.CompilerParams(
            collective_id=0, has_side_effects=True, vmem_limit_bytes=60 * 1024 * 1024
        ),
    )(
        layer_input,
        norm_gain.reshape(-1, 128),
        query_base,
        query_down.T,
        query_up,
        kv_base,
        output_base_weight,
        output_down_factor.T,
        output_up_factor,
        cache_keys[0],
        cache_values[0],
        positions,
        offsets,
    )


def solution(mesh):
    in_specs = (
        P(("engine", "fsdp"), "tensor"),
        P("tensor"),
        P(("engine", "fsdp"), "tensor"),
        P(("engine", "fsdp"), None),
        P(None, "tensor"),
        P("tensor", ("engine", "fsdp"), None),
        P(None, "tensor", ("engine", "fsdp")),
        P("tensor", None),
        P(None, "tensor", ("engine", "fsdp")),
        P(("engine", "fsdp"), None, None),
        P(("engine", "fsdp"), None, None),
        P(("engine", "fsdp"), None),
        P(("engine", "fsdp")),
    )
    out_specs = P(("engine", "fsdp"), "tensor")
    shape = dict(mesh.shape)
    paired = shape["tensor"] == 2 and shape["engine"] == 4
    body = functools.partial(per_device, shape["fsdp"]) if paired else per_device_plain
    return jax.shard_map(
        body, mesh=mesh, in_specs=in_specs, out_specs=out_specs, check_vma=False
    )
```

```python
import functools

import jax
import jax.numpy as jnp
from jax import lax
from jax.experimental import pallas as pl
from jax.experimental.pallas import tpu as pltpu
from jax.sharding import PartitionSpec as P

MESH = pl.DeviceIdType.MESH
KV, QUERY, OUT = 0, 1, 2
SIB, CROSS, LEFT, RIGHT = 0, 1, 2, 3


def rotate(values, places):
    half = values.shape[-1] // 2
    index = jnp.arange(half).astype(jnp.float32)
    inverse = jnp.exp(index * (-2.0 / values.shape[-1]) * jnp.log(jnp.float32(500000.0)))
    angle = places.astype(jnp.float32)[:, None] * inverse[None, :]
    cosine = jnp.cos(angle)
    sine = jnp.sin(angle)
    first = values[:, :half]
    second = values[:, half:]
    return jnp.concatenate([first * cosine - second * sine, second * cosine + first * sine], axis=1)


def attend(query, new_keys, new_values, old_keys, old_values, offset):
    tok_count = query.shape[0]
    slots = old_keys.shape[0]
    keys_all = jnp.concatenate([old_keys, new_keys], axis=0)
    values_all = jnp.concatenate([old_values, new_values], axis=0)
    scores = jnp.dot(query, keys_all.T, preferred_element_type=jnp.float32) * query.shape[-1] ** (
        -0.5
    )
    slot_seen = jnp.broadcast_to(jnp.arange(slots)[None, :] < offset, (tok_count, slots))
    rows = jnp.arange(tok_count)
    new_seen = rows[None, :] <= rows[:, None]
    seen = jnp.concatenate([slot_seen, new_seen], axis=1)
    scores = jnp.where(seen, scores, jnp.float32(-1e30))
    top = jnp.max(scores, axis=1, keepdims=True)
    probs = jnp.exp(scores - top)
    weights = (probs / jnp.sum(probs, axis=1, keepdims=True)).astype(jnp.bfloat16)
    return jnp.dot(weights, values_all, preferred_element_type=jnp.float32).astype(jnp.bfloat16)


def per_device_plain(
    layer_input,
    norm_gain,
    query_base,
    query_down,
    query_up,
    kv_base,
    output_base_weight,
    output_down_factor,
    output_up_factor,
    cache_keys,
    cache_values,
    positions,
    offsets,
):
    head_size = query_base.shape[1]
    tok_count = layer_input.shape[0]
    full_input, full_gain, complete_down_factor = (
        lax.all_gather(layer_input, "tensor", axis=1, tiled=True),
        lax.all_gather(norm_gain, "tensor", axis=0, tiled=True),
        lax.all_gather(output_down_factor, "tensor", axis=0, tiled=True),
    )
    wide = full_input.astype(jnp.float32)
    scale = lax.rsqrt(jnp.mean(wide * wide, axis=1, keepdims=True) + 1e-05)
    normed = (wide * scale * full_gain.astype(jnp.float32)[None, :]).astype(jnp.bfloat16)
    local_normed = (
        layer_input.astype(jnp.float32) * scale * norm_gain.astype(jnp.float32)[None, :]
    ).astype(jnp.bfloat16)
    merged_query = (
        query_base.astype(jnp.float32)
        + 2.0 * jnp.dot(query_down, query_up, preferred_element_type=jnp.float32)
    ).astype(jnp.bfloat16)
    columns = normed
    query_raw = jnp.dot(
        columns,
        lax.all_gather(merged_query, ("engine", "fsdp"), axis=0, tiled=True),
        preferred_element_type=jnp.float32,
    )
    columns = local_normed
    kv_part = jnp.dot(
        columns,
        lax.all_gather(kv_base, ("engine", "fsdp"), axis=1, tiled=True)[0],
        preferred_element_type=jnp.float32,
    )
    kv_total = lax.psum(kv_part.astype(jnp.bfloat16), "tensor").astype(jnp.float32)
    places = positions[0]
    query = rotate(query_raw, places).astype(jnp.bfloat16)
    new_keys = rotate(kv_total[:, :head_size], places).astype(jnp.bfloat16)
    new_values = kv_total[:, head_size:].astype(jnp.bfloat16)
    head_out = attend(query, new_keys, new_values, cache_keys[0], cache_values[0], offsets[0])
    adapter_output_delta = jnp.einsum(
        "lz,zam->lam",
        complete_down_factor.astype(jnp.float32),
        output_up_factor.astype(jnp.float32),
    )
    combined_output_weight = (
        output_base_weight.astype(jnp.float32) + 2.0 * adapter_output_delta
    ).astype(jnp.bfloat16)
    own_rows = lax.all_to_all(
        combined_output_weight, "tensor", split_axis=0, concat_axis=1, tiled=True
    )
    terms = jnp.einsum(
        "tk,kbn->tbn",
        head_out,
        lax.all_gather(own_rows, ("engine", "fsdp"), axis=2, tiled=True),
        preferred_element_type=jnp.float32,
    )
    flat_terms = terms.reshape(tok_count, terms.shape[1] * terms.shape[2])
    attended = lax.psum_scatter(
        flat_terms.astype(jnp.bfloat16), "tensor", scatter_dimension=1, tiled=True
    )
    return attended


def kernel(
    n_f,
    input_hbm,
    gain_hbm,
    qbase_hbm,
    qdown_hbm,
    qup_hbm,
    kvbase_hbm,
    obase_hbm,
    odown_hbm,
    oup_hbm,
    ckeys_hbm,
    cvalues_hbm,
    places_hbm,
    offset_ref,
    result_ref,
    input_ref,
    gain_ref,
    qbase_ref,
    qdown_ref,
    qup_ref,
    obase_ref,
    odown_ref,
    oup_ref,
    ckeys_ref,
    cvalues_ref,
    places_ref,
    kv_buf,
    q_buf,
    o_buf,
    normed,
    squares,
    down_full,
    kv_part,
    q_total,
    heads,
    both,
    cosine_ref,
    sine_ref,
    recv_sem,
    send_sem,
    y_recv,
    y_send,
    n_recv,
    n_send,
    load_sem,
    out_buf,
    out_sem,
):
    engine = lax.axis_index("engine")
    z = lax.axis_index("fsdp")
    t = lax.axis_index("tensor")
    core = lax.rem(engine, 2)
    sibling = engine + 1 - 2 * core
    across = lax.rem(engine + 2, 4)
    other = 1 - t
    bufs = (kv_buf, q_buf, o_buf)
    groups = 4 * n_f
    tok = input_ref.shape[0]
    head = qbase_ref.shape[1]
    piece = kvbase_hbm.shape[0]
    half_groups = groups // 2
    mine = engine * n_f + z
    width = 2 * input_ref.shape[1]

    def copy(m, g, way):
        target = {
            SIB: (sibling, z, t),
            CROSS: (across, z, t),
            LEFT: (engine, jnp.maximum(z - 1, 0), t),
            RIGHT: (engine, jnp.minimum(z + 1, n_f - 1), t),
        }[way]
        return pltpu.make_async_remote_copy(
            src_ref=bufs[m].at[g],
            dst_ref=bufs[m].at[g],
            send_sem=send_sem.at[m, way, g],
            recv_sem=recv_sem.at[m, g],
            device_id=target,
            device_id_type=MESH,
        )

    def to_partner(ref, k):
        return pltpu.make_async_remote_copy(
            src_ref=ref.at[t],
            dst_ref=ref.at[t],
            send_sem=y_send.at[k],
            recv_sem=y_recv.at[k],
            device_id=(engine, z, other),
            device_id_type=MESH,
        )

    def from_partner(ref, k):
        return pltpu.make_async_remote_copy(
            src_ref=ref.at[other],
            dst_ref=ref.at[other],
            send_sem=y_send.at[k],
            recv_sem=y_recv.at[k],
            device_id=(engine, z, other),
            device_id_type=MESH,
        )

    def normed_copy(side, k):
        rows = normed.at[pl.ds(side * groups + 2 * k, 2)]
        return pltpu.make_async_remote_copy(
            src_ref=rows,
            dst_ref=rows,
            send_sem=n_send.at[k],
            recv_sem=n_recv.at[k],
            device_id=(engine, z, other),
            device_id_type=MESH,
        )

    def own(m):
        g = engine * n_f + z
        copy(m, g, CROSS).start()

        @pl.when(z > 0)
        def _():
            copy(m, g, LEFT).start()

        @pl.when(z < n_f - 1)
        def _():
            copy(m, g, RIGHT).start()

        copy(m, g, SIB).start()

    def along(m, d):
        @pl.when(z >= d)
        def _():
            g = engine * n_f + z - d
            copy(m, g, SIB).wait_recv()

            @pl.when(z < n_f - 1)
            def _():
                copy(m, g, RIGHT).start()

            copy(m, g, CROSS).start()
            copy(m, g, SIB).start()

        @pl.when(z + d < n_f)
        def _():
            g = engine * n_f + z + d
            copy(m, g, SIB).wait_recv()

            @pl.when(z > 0)
            def _():
                copy(m, g, LEFT).start()

            copy(m, g, CROSS).start()
            copy(m, g, SIB).start()

    def crossing(m, d):
        def take(zz):
            g = across * n_f + zz
            copy(m, g, SIB).wait_recv()
            copy(m, g, SIB).start()

        if d == 0:
            take(z)
        else:
            pl.when(z >= d)(lambda: take(z - d))
            pl.when(z + d < n_f)(lambda: take(z + d))

    def from_sibling(m):
        def arrived(k, carry):
            copy(m, sibling * n_f + k, SIB).wait_recv()
            copy(m, lax.rem(sibling + 2, 4) * n_f + k, SIB).wait_recv()
            return carry

        lax.fori_loop(0, n_f, arrived, 0)

    loads = [
        pltpu.make_async_copy(source, target, load_sem.at[k])
        for k, (source, target) in enumerate(
            (
                (kvbase_hbm, kv_buf.at[mine]),
                (odown_hbm, odown_ref),
                (input_hbm, input_ref),
                (qbase_hbm, qbase_ref),
                (qdown_hbm, qdown_ref),
                (qup_hbm, qup_ref),
                (gain_hbm, gain_ref),
                (obase_hbm, obase_ref),
                (oup_hbm, oup_ref),
                (places_hbm, places_ref),
                (ckeys_hbm, ckeys_ref),
                (cvalues_hbm, cvalues_ref),
            )
        )
    ]
    for load in loads:
        load.start()

    barrier = pltpu.get_barrier_semaphore()

    def greet(target):
        pl.semaphore_signal(barrier, inc=1, device_id=target, device_id_type=MESH)

    greet((sibling, z, t))
    greet((across, z, t))
    greet((engine, z, other))
    pl.when(z > 0)(lambda: greet((engine, z - 1, t)))
    pl.when(z < n_f - 1)(lambda: greet((engine, z + 1, t)))

    loads[0].wait()
    loads[1].wait()
    down_full[t] = odown_ref[...]
    pl.semaphore_wait(barrier, 5 - (z == 0).astype(jnp.int32) - (z == n_f - 1).astype(jnp.int32))

    own(KV)
    to_partner(down_full, 1).start()
    loads[2].wait()
    total = jnp.zeros((tok, 128), jnp.float32)
    for k in range(input_ref.shape[1] // 128):
        wide = input_ref[:, k * 128 : (k + 1) * 128].astype(jnp.float32)
        total = total + wide * wide
    squares[t] = total
    to_partner(squares, 0).start()

    over_rank = (((0,), (0,)), ((), ()))
    for k in range(3, 6):
        loads[k].wait()
    q_buf[mine] = (
        qbase_ref[...].astype(jnp.float32)
        + 2.0
        * lax.dot_general(
            qdown_ref[...], qup_ref[...], over_rank, preferred_element_type=jnp.float32
        )
    ).astype(jnp.bfloat16)
    own(QUERY)

    loads[6].wait()
    from_partner(squares, 0).wait_recv()
    mean = jnp.sum(squares[0] + squares[1], axis=1, keepdims=True) * (1.0 / width)
    scale = jnp.broadcast_to(lax.rsqrt(mean + 1e-05), (tok, 128))
    each = piece // 128
    for k in range(groups):
        for part in range(each):
            at = k * each + part
            normed[t * groups + k, :, part * 128 : (part + 1) * 128] = (
                input_ref[:, at * 128 : (at + 1) * 128].astype(jnp.float32)
                * scale
                * gain_ref[at : at + 1, :].astype(jnp.float32)
            ).astype(jnp.bfloat16)
        if k % 2 == 1:
            normed_copy(t, k // 2).start()

    for k in range(7, len(loads)):
        loads[k].wait()

    along(KV, 1)
    along(KV, 2)

    from_partner(down_full, 1).wait_recv()
    for side in range(2):
        rows = slice(side * head, (side + 1) * head)
        o_buf[mine, rows, :] = (
            obase_ref[rows, :].astype(jnp.float32)
            + 2.0
            * lax.dot_general(
                down_full[side], oup_ref[...], over_rank, preferred_element_type=jnp.float32
            )
        ).astype(jnp.bfloat16)
    own(OUT)

    along(QUERY, 1)
    along(KV, 3)
    crossing(KV, 0)

    lane = lax.broadcasted_iota(jnp.int32, (tok, head), 1)
    low = lane < head // 2
    index = jnp.where(low, lane, lane - head // 2).astype(jnp.float32)
    inverse = jnp.exp(index * (-2.0 / head) * jnp.log(jnp.full((tok, head), 500000.0, jnp.float32)))
    places = jnp.broadcast_to(places_ref[...].astype(jnp.float32), (head, tok)).T
    angle = places * inverse
    cosine_ref[...] = jnp.cos(angle)
    sine_ref[...] = jnp.where(low, -jnp.sin(angle), jnp.sin(angle))

    def rope(values):
        return values * cosine_ref[...] + pltpu.roll(values, head // 2, 1) * sine_ref[...]

    along(QUERY, 2)
    crossing(KV, 1)
    along(QUERY, 3)
    crossing(KV, 2)
    along(OUT, 1)
    crossing(KV, 3)
    crossing(QUERY, 0)
    along(OUT, 2)
    from_sibling(KV)
    kv_part[t] = jnp.zeros(kv_part.shape[1:], jnp.float32)

    def kv_step(g, carry):
        kv_part[t] += jnp.dot(
            normed[t * groups + g], kv_buf[g], preferred_element_type=jnp.float32
        )
        return carry

    lax.fori_loop(0, groups // 2, kv_step, 0)
    crossing(QUERY, 1)
    along(OUT, 3)
    lax.fori_loop(groups // 2, groups, kv_step, 0)
    to_partner(kv_part, 2).start()

    q_total[...] = jnp.zeros_like(q_total)
    local = engine // 2 == t

    def q_step(g):
        @pl.when(g // half_groups != t)
        def _():
            normed_copy(other, lax.rem(g, half_groups)).wait_recv()

        q_total[...] += jnp.dot(
            normed[2 * g], q_buf[g, :piece, :], preferred_element_type=jnp.float32
        ) + jnp.dot(normed[2 * g + 1], q_buf[g, piece:, :], preferred_element_type=jnp.float32)

    def q_column():
        def step(k, carry):
            q_step(engine * n_f + k)
            g = sibling * n_f + k
            copy(QUERY, g, SIB).wait_recv()
            q_step(g)
            return carry

        lax.fori_loop(0, n_f, step, 0)

    def q_crossed(d):
        def pair(zz):
            q_step(across * n_f + zz)
            g = lax.rem(sibling + 2, 4) * n_f + zz
            copy(QUERY, g, SIB).wait_recv()
            q_step(g)

        if d == 0:
            pair(z)
        else:
            pl.when(z >= d)(lambda: pair(z - d))
            pl.when(z + d < n_f)(lambda: pair(z + d))

    def q_first():
        q_crossed(0)
        q_crossed(1)

    pl.when(local)(q_column)
    pl.when(jnp.logical_not(local))(q_first)
    crossing(QUERY, 2)
    pl.when(local)(q_first)
    pl.when(jnp.logical_not(local))(q_column)
    crossing(QUERY, 3)
    crossing(OUT, 0)
    q_crossed(2)
    q_crossed(3)

    query = rope(q_total[...]).astype(jnp.bfloat16)
    from_partner(kv_part, 2).wait_recv()
    kv = kv_part[0] + kv_part[1]
    new_keys = rope(kv[:, :head]).astype(jnp.bfloat16)
    new_values = kv[:, head:].astype(jnp.bfloat16)
    dims = (((1,), (1,)), ((), ()))
    slots = ckeys_ref.shape[0]
    factor = head ** (-0.5)
    old = lax.dot_general(query, ckeys_ref[...], dims, preferred_element_type=jnp.float32) * factor
    new = lax.dot_general(query, new_keys, dims, preferred_element_type=jnp.float32) * factor
    seen = lax.broadcasted_iota(jnp.int32, (tok, slots), 1) < offset_ref[0]
    rows = lax.broadcasted_iota(jnp.int32, (tok, tok), 0)
    columns = lax.broadcasted_iota(jnp.int32, (tok, tok), 1)
    old = jnp.where(seen, old, jnp.float32(-1e30))
    new = jnp.where(columns <= rows, new, jnp.float32(-1e30))
    top = jnp.maximum(
        jnp.max(old, axis=1, keepdims=True), jnp.max(new, axis=1, keepdims=True)
    )
    old = jnp.exp(old - top)
    new = jnp.exp(new - top)
    summed = jnp.sum(old, axis=1, keepdims=True) + jnp.sum(new, axis=1, keepdims=True)
    old = (old / summed).astype(jnp.bfloat16)
    new = (new / summed).astype(jnp.bfloat16)
    own_head = (
        jnp.dot(old, cvalues_ref[...], preferred_element_type=jnp.float32)
        + jnp.dot(new, new_values, preferred_element_type=jnp.float32)
    ).astype(jnp.bfloat16)
    heads[t] = own_head
    to_partner(heads, 3).start()
    crossing(OUT, 1)
    from_partner(heads, 3).wait_recv()

    both[:, :head] = heads[0]
    both[:, head:] = heads[1]

    def written(g):
        return pltpu.make_async_copy(
            out_buf.at[g],
            result_ref.at[:, pl.ds(pl.multiple_of(g * piece, piece), piece)],
            out_sem.at[g],
        )

    def project(g):
        out_buf[g] = jnp.dot(
            both[...], o_buf[g], preferred_element_type=jnp.float32
        ).astype(jnp.bfloat16)
        written(g).start()

    def near(k, carry):
        project(engine * n_f + k)
        g = sibling * n_f + k
        copy(OUT, g, SIB).wait_recv()
        project(g)
        return carry

    def crossed(d):
        def pair(zz):
            project(across * n_f + zz)
            g = lax.rem(sibling + 2, 4) * n_f + zz
            copy(OUT, g, SIB).wait_recv()
            project(g)

        if d == 0:
            pair(z)
        else:
            pl.when(z >= d)(lambda: pair(z - d))
            pl.when(z + d < n_f)(lambda: pair(z + d))

    lax.fori_loop(0, n_f, near, 0)
    crossing(OUT, 2)
    crossed(0)
    crossed(1)
    crossing(OUT, 3)
    crossed(2)
    crossed(3)

    for m in range(3):

        def drain(k, carry, m=m):
            g = engine * n_f + k
            copy(m, g, SIB).wait_send()
            copy(m, g, CROSS).wait_send()
            copy(m, across * n_f + k, SIB).wait_send()

            @pl.when((z > 0) & (k >= z))
            def _():
                copy(m, g, LEFT).wait_send()

            @pl.when((z < n_f - 1) & (k <= z))
            def _():
                copy(m, g, RIGHT).wait_send()

            return carry

        lax.fori_loop(0, n_f, drain, 0)

    def drain_normed(k, carry):
        normed_copy(t, k).wait_send()
        return carry

    lax.fori_loop(0, half_groups, drain_normed, 0)

    def drain_out(g, carry):
        written(g).wait()
        return carry

    lax.fori_loop(0, groups, drain_out, 0)
    to_partner(squares, 0).wait_send()
    to_partner(down_full, 1).wait_send()
    to_partner(kv_part, 2).wait_send()
    to_partner(heads, 3).wait_send()


def per_device(
    n_f,
    layer_input,
    norm_gain,
    query_base,
    query_down,
    query_up,
    kv_base,
    output_base_weight,
    output_down_factor,
    output_up_factor,
    cache_keys,
    cache_values,
    positions,
    offsets,
):
    tok, features = layer_input.shape
    depth, head = query_base.shape
    rank = query_up.shape[0]
    groups = 4 * n_f
    kv_base = kv_base[0]
    output_base_weight = output_base_weight[:, 0]
    output_up_factor = output_up_factor[:, 0]
    piece = kv_base.shape[0]
    hbm = pl.BlockSpec(memory_space=pltpu.HBM)
    smem = pl.BlockSpec(memory_space=pltpu.SMEM)
    dma = pltpu.SemaphoreType.DMA
    return pl.pallas_call(
        functools.partial(kernel, n_f),
        out_shape=jax.ShapeDtypeStruct((tok, features), jnp.bfloat16),
        in_specs=[hbm] * 12 + [smem],
        out_specs=hbm,
        scratch_shapes=[
            pltpu.VMEM((tok, features), jnp.bfloat16),
            pltpu.VMEM((features // 128, 128), jnp.bfloat16),
            pltpu.VMEM(query_base.shape, jnp.bfloat16),
            pltpu.VMEM((rank, depth), jnp.bfloat16),
            pltpu.VMEM(query_up.shape, jnp.bfloat16),
            pltpu.VMEM(output_base_weight.shape, jnp.bfloat16),
            pltpu.VMEM((rank, head), jnp.bfloat16),
            pltpu.VMEM(output_up_factor.shape, jnp.bfloat16),
            pltpu.VMEM(cache_keys.shape[1:], jnp.bfloat16),
            pltpu.VMEM(cache_values.shape[1:], jnp.bfloat16),
            pltpu.VMEM(positions.shape, jnp.int32),
            pltpu.VMEM((groups,) + kv_base.shape, jnp.bfloat16),
            pltpu.VMEM((groups,) + query_base.shape, jnp.bfloat16),
            pltpu.VMEM((groups,) + output_base_weight.shape, jnp.bfloat16),
            pltpu.VMEM((2 * groups, tok, piece), jnp.bfloat16),
            pltpu.VMEM((2, tok, 128), jnp.float32),
            pltpu.VMEM((2, rank, head), jnp.bfloat16),
            pltpu.VMEM((2, tok, 2 * head), jnp.float32),
            pltpu.VMEM((tok, head), jnp.float32),
            pltpu.VMEM((2, tok, head), jnp.bfloat16),
            pltpu.VMEM((tok, 2 * head), jnp.bfloat16),
            pltpu.VMEM((tok, head), jnp.float32),
            pltpu.VMEM((tok, head), jnp.float32),
            dma((3, groups)),
            dma((3, 4, groups)),
            dma((4,)),
            dma((4,)),
            dma((groups // 2,)),
            dma((groups // 2,)),
            dma((12,)),
            pltpu.VMEM((groups, tok, piece), jnp.bfloat16),
            dma((groups,)),
        ],
        compiler_params=pltpu.CompilerParams(
            collective_id=0, has_side_effects=True, vmem_limit_bytes=60 * 1024 * 1024
        ),
    )(
        layer_input,
        norm_gain.reshape(-1, 128),
        query_base,
        query_down.T,
        query_up,
        kv_base,
        output_base_weight,
        output_down_factor.T,
        output_up_factor,
        cache_keys[0],
        cache_values[0],
        positions,
        offsets,
    )


def solution(mesh):
    in_specs = (
        P(("engine", "fsdp"), "tensor"),
        P("tensor"),
        P(("engine", "fsdp"), "tensor"),
        P(("engine", "fsdp"), None),
        P(None, "tensor"),
        P("tensor", ("engine", "fsdp"), None),
        P(None, "tensor", ("engine", "fsdp")),
        P("tensor", None),
        P(None, "tensor", ("engine", "fsdp")),
        P(("engine", "fsdp"), None, None),
        P(("engine", "fsdp"), None, None),
        P(("engine", "fsdp"), None),
        P(("engine", "fsdp")),
    )
    out_specs = P(("engine", "fsdp"), "tensor")
    shape = dict(mesh.shape)
    paired = shape["tensor"] == 2 and shape["engine"] == 4
    body = functools.partial(per_device, shape["fsdp"]) if paired else per_device_plain
    return jax.shard_map(
        body, mesh=mesh, in_specs=in_specs, out_specs=out_specs, check_vma=False
    )
```
